256 devices in a mesh: lon: 16 (over x, y), lat: 16 (over z, core).
Axes of the slice: x: 4, y: 4, z: 8, core: 2. Of those that a mesh axis runs over, the one named last changes fastest.
Arguments:
- tracer: float32 [4096, 128, 128], P('lon', 'lat'), may hold values from -6 to 6
- offsets: int32 [128], P('lat'), may hold values from 0 to 4095
- frac_lon: float32 [128], P('lat'), may hold values from 0 to 1
- frac_lat: float32 [128], P('lat'), may hold values from 0 to 1
- frac_lev: float32 [128], P('lat'), may hold values from 0 to 1
- metric: float32 [128], P('lat'), may hold values from 0.5 to 2
- vertical_coef: float32 [128], replicated, may hold values from 0.5 to 4
- inverses: float32 [128, 128, 128], P('lat'), may hold values from -0.1 to 0.6, as said below
Outputs:
- advected: float32 [4096, 128, 128], P('lon', 'lat')
- pressure: float32 [4096, 128, 128], P('lon', 'lat')
- residual: float32 [4096, 128, 128], P('lon', 'lat')
The draws below stay inside these ranges and needn't reach their ends.
Inputs may be any that keep to these rules, and one draw needn't show every extreme that they name: `inverses`: one matrix for each latitude row.
All inputs are finite; a program needn't handle non-finite values.
Results may differ from the reference program's by a relative error of at most 0.00016.
Values sent between devices are 32-bit elements; how exact they have to be, the bound alone decides.
No kernel may reach another device: no remote copies, remote signals or barrier semaphores. Data moves between devices by JAX's collectives and lax.ppermute only.
A program may use at most 128 MiB of HBM per device.

```python
import math
import jax
import jax.numpy as jnp
from jax import lax

L = 128
ITERS = 3
NX = 4096
NY = 128


def draw_inverses(key, part):
    first_key, second_key = jax.random.split(jax.random.fold_in(key, 7))
    scales = jnp.exp(jax.random.uniform(first_key, (NY,), jnp.float32, jnp.log(0.1), jnp.log(0.5)))
    noise = jnp.clip(jax.random.normal(second_key, (NY, L, L), jnp.float32), -3.0, 3.0)
    identity = jnp.eye(L, dtype=jnp.float32)
    return scales[:, None, None] * (identity[None] + 0.03 * noise)


def set_ends(entries, rng, least, top_value):
    longest = entries.shape.index(max(entries.shape))
    spots = []
    for shift in (0, 1):
        where = [jax.random.randint(jax.random.fold_in(rng, axis), (), 0, length) for axis, length in enumerate(entries.shape)]
        where[longest] = (where[longest] + shift) % entries.shape[longest]
        spots.append(tuple(where))
    return entries.at[spots[0]].set(least).at[spots[1]].set(top_value)


def steps_of(own_key, extent, shards, least, largest):
    loudness = 1.0
    for dim, blocks in shards:
        draws = jax.random.uniform(jax.random.fold_in(jax.random.fold_in(own_key, 6), dim), (blocks,), jnp.float32, least / len(shards), largest / len(shards))
        loudness = loudness * jnp.repeat(jnp.exp(draws), extent[dim] // blocks).reshape((-1,) + (1,) * (len(extent) - 1 - dim))
    return loudness


def normal_values(rng, extent, spread, limit, cuts=(), held_as=jnp.bfloat16):
    entries = jax.random.normal(rng, extent, jnp.float32) * spread
    if len(cuts) > 0:
        entries = steps_of(rng, extent, cuts, -0.22, 0.18) * entries
    return jnp.clip(entries, min=-limit, max=limit).astype(held_as)


def setup_inputs(seed: int = 0) -> dict:
    arg_keys = jax.random.split(jax.random.key(seed), 9)
    tracer = normal_values(arg_keys[0], (NX, NY, L), 1.0, 6.0, ((0, 16), (1, 16)), jnp.float32)
    offsets = set_ends(jax.random.randint(arg_keys[1], (NY,), 0, NX), jax.random.fold_in(arg_keys[1], 1), 0, NX - 1).astype(jnp.int32)
    frac_lon = jnp.clip(1.0 * jax.random.uniform(arg_keys[2], (NY,), jnp.float32) ** steps_of(arg_keys[2], (NY,), ((0, 16),), -0.2, 0.2), 0.0, 1.0)
    frac_lat = jnp.clip(1.0 * jax.random.uniform(arg_keys[3], (NY,), jnp.float32) ** steps_of(arg_keys[3], (NY,), ((0, 16),), -0.2, 0.2), 0.0, 1.0)
    frac_lev = jnp.clip(1.0 * jax.random.uniform(arg_keys[4], (NY,), jnp.float32) ** steps_of(arg_keys[4], (NY,), ((0, 16),), -0.2, 0.2), 0.0, 1.0)
    metric = jnp.clip(jnp.exp(math.log(2.0) - 1.3862944 * jax.random.uniform(arg_keys[5], (NY,), jnp.float32) ** steps_of(arg_keys[5], (NY,), ((0, 16),), -0.2, 0.2)), 0.5, 2.0)
    vertical_coef = jnp.clip(jnp.exp(jax.random.uniform(arg_keys[6], (L,), jnp.float32, math.log(0.5), math.log(4.0))), 0.5, 4.0)
    inverses = draw_inverses(jax.random.fold_in(arg_keys[8], 71), 0)
    return {"tracer": tracer, "offsets": offsets, "frac_lon": frac_lon, "frac_lat": frac_lat, "frac_lev": frac_lev, "metric": metric, "vertical_coef": vertical_coef, "inverses": inverses}


def cubic_weights(fraction):
    return (-fraction * (fraction - 1.0) * (fraction - 2.0) / 6.0,
            (fraction + 1.0) * (fraction - 1.0) * (fraction - 2.0) / 2.0,
            -(fraction + 1.0) * fraction * (fraction - 2.0) / 2.0,
            (fraction + 1.0) * fraction * (fraction - 1.0) / 6.0)


def operate(field, metric, vertical_coef):
    eastern = jnp.roll(field, -1, 0)
    western = jnp.roll(field, 1, 0)
    padded = jnp.pad(field, ((0, 0), (1, 1), (0, 0)))
    levels = jnp.pad(field, ((0, 0), (0, 0), (1, 1)))
    result = metric[None, :, None] * (2.0 * field - eastern - western)
    result = result + (2.0 * field - padded[:, 2:] - padded[:, :-2])
    result = result + vertical_coef[None, None, :] * (2.0 * field - levels[:, :, 2:] - levels[:, :, :-2])
    return result + 0.1 * field


def precondition(inverses, field):
    return jnp.einsum('jkm,xjm->xjk', inverses, field, precision=lax.Precision.HIGHEST)


def reference(tracer, offsets, frac_lon, frac_lat, frac_lev, metric, vertical_coef, inverses):
    lat_weights = cubic_weights(frac_lat)
    padded = jnp.pad(tracer, ((0, 0), (1, 2), (0, 0)))
    lat_mixed = jnp.zeros_like(tracer)
    for tap_index in range(4):
        lat_mixed = lat_mixed + lat_weights[tap_index][None, :, None] * padded[:, tap_index:tap_index + NY]
    lev_weights = cubic_weights(frac_lev)
    padded = jnp.pad(lat_mixed, ((0, 0), (0, 0), (1, 2)))
    lev_mixed = jnp.zeros_like(tracer)
    for tap_index in range(4):
        lev_mixed = lev_mixed + lev_weights[tap_index][None, :, None] * padded[:, :, tap_index:tap_index + L]
    lon_weights = cubic_weights(frac_lon)
    columns = jnp.arange(NX, dtype=jnp.int32)[:, None]
    row_index = jnp.arange(NY, dtype=jnp.int32)[None, :]
    advected = jnp.zeros_like(tracer)
    for tap_index in range(4):
        source = jnp.mod(columns - offsets.astype(jnp.int32)[None, :] + (tap_index - 1), NX).astype(jnp.int32)
        advected = advected + lon_weights[tap_index][None, :, None] * lev_mixed[source, row_index]
    pressure = jnp.zeros_like(advected)
    residual = advected
    first = precondition(inverses, residual)
    directions = [first]
    images = [operate(first, metric, vertical_coef)]
    along = jnp.sum(residual * images[0])
    squares = [jnp.sum(images[0] * images[0])]
    for step in range(ITERS):
        alpha = along / squares[step]
        pressure = pressure + alpha * directions[step]
        residual = residual - alpha * images[step]
        if step + 1 < ITERS:
            search = precondition(inverses, residual)
            image_new = operate(search, metric, vertical_coef)
            direction_new = search
            for prior in range(step + 1):
                factor = -jnp.sum(image_new * images[prior]) / squares[prior]
                direction_new = direction_new + factor * directions[prior]
                image_new = image_new + factor * images[prior]
            directions.append(direction_new)
            images.append(image_new)
            along = jnp.sum(residual * image_new)
            squares.append(jnp.sum(image_new * image_new))
    return advected, pressure, residual
```

```python
import functools

import jax
import jax.numpy as jnp
from jax import lax
from jax.experimental import pallas as pl
from jax.experimental.pallas import tpu as pltpu
from jax.sharding import Mesh
from jax.sharding import PartitionSpec as P

LON = ("lon_0", "lon_1")
LAT = ("lat_0", "lat_1")
LON_LAT = ("lon_0", "lon_1", "lat_0", "lat_1")
W = 256
R = 8
L = 128
H = 3
E = W + 8
NL = 16
MIB = 1 << 20


def weights(f):
    sixth = 1.0 / 6.0
    return (
        -f * (f - 1.0) * (f - 2.0) * sixth,
        (f + 1.0) * (f - 1.0) * (f - 2.0) * 0.5,
        -(f + 1.0) * f * (f - 2.0) * 0.5,
        (f + 1.0) * f * (f - 1.0) * sixth,
    )


def halves(x):
    high = x.astype(jnp.bfloat16)
    return high, (x - high.astype(jnp.float32)).astype(jnp.bfloat16)


def dot_nt(a, b):
    return lax.dot_general(
        a, b, (((1,), (1,)), ((), ())), preferred_element_type=jnp.float32
    )


def row_of(j):
    return pl.ds(j, W, stride=R)


def edges_kernel(tracer, inverses, metric, up, down, up_inv, down_inv):
    up[...] = tracer[row_of(R - 1), :]
    down[0:W, :] = tracer[row_of(0), :]
    down[W : 2 * W, :] = tracer[row_of(1), :]
    for i in range(H):
        up_inv[i * L : (i + 1) * L, :] = inverses[R - H + i]
        down_inv[i * L : (i + 1) * L, :] = inverses[i]
    sub = lax.broadcasted_iota(jnp.int32, (8, L), 0)
    for ref, first in ((up_inv, R - H), (down_inv, 0)):
        tile = jnp.zeros((8, L), jnp.float32)
        for i in range(H):
            tile = jnp.where(sub == i, metric[first + i], tile)
        ref[H * L : H * L + 8, :] = tile


def mix_kernel(frac_lat, frac_lev, tracer, south, north, out):
    delta = lax.broadcasted_iota(jnp.int32, (L, L), 1) - lax.broadcasted_iota(
        jnp.int32, (L, L), 0
    )

    def row(k):
        if k < 0:
            return south[...]
        if k >= R:
            return north[(k - R) * W : (k - R + 1) * W, :]
        return tracer[row_of(k), :]

    for j in range(R):
        w = weights(frac_lat[j])
        mixed = w[0] * row(j - 1) + w[1] * row(j) + w[2] * row(j + 1) + w[3] * row(j + 2)
        v = weights(frac_lev[j])
        table = jnp.zeros((L, L), jnp.float32)
        for m in range(4):
            table = jnp.where(delta == m - 1, v[m], table)
        t_high, t_low = halves(table)
        m_high, m_low = halves(mixed)
        left = jnp.concatenate(
            [
                jnp.concatenate([t_high, t_high], 1),
                jnp.concatenate([t_low, t_low], 1),
            ],
            0,
        )
        both = dot_nt(left, jnp.concatenate([m_high, m_low], 1))
        turned = (both[:L] + both[L:]).reshape(NL, 8, W)
        out[:, 0, j] = turned[:, :, :128]
        out[:, 1, j] = turned[:, :, 128:]


def shift_kernel(offsets, frac_lon, cells, out, spun):
    lane = lax.broadcasted_iota(jnp.int32, (8, 128), 1)
    blocks = 2 * NL
    for j in range(R):
        w = weights(frac_lon[j])
        off = offsets[j]
        turns = lax.shift_right_logical(off, 7)
        rest = jnp.bitwise_and(off, 127)
        for b in range(blocks):
            here = cells[b, j]
            before = cells[(b - 1) % blocks, j]
            after = cells[(b + 1) % blocks, j]
            west = pltpu.roll(jnp.where(lane == 127, before, here), 1, 1)
            east = pltpu.roll(jnp.where(lane == 0, after, here), 127, 1)
            far = pltpu.roll(jnp.where(lane < 2, after, here), 126, 1)
            value = w[0] * west + w[1] * here + w[2] * east + w[3] * far
            spun[b, j] = pltpu.roll(value, rest, 1)
        moved = []
        for b in range(blocks):
            near = spun[jnp.bitwise_and(b - turns, blocks - 1), j]
            past = spun[jnp.bitwise_and(b - turns - 1, blocks - 1), j]
            moved.append(jnp.where(lane >= rest, near, past))
        for d in range(NL):
            out[d, j] = moved[2 * d]
            out[d, R + j] = moved[2 * d + 1]
            rim = jnp.where(
                lane < 4,
                moved[(2 * d + 2) % blocks],
                pltpu.roll(moved[(2 * d - 1) % blocks], 8, 1),
            )
            if j == 0:
                out[d, 2 * R] = jnp.where(lane < 8, rim, 0.0)
            else:
                rim = pltpu.roll(rim, 8 * j, 1)
                slot = (lane >= 8 * j) & (lane < 8 * j + 8)
                out[d, 2 * R] = jnp.where(slot, rim, out[d, 2 * R])


def turn_kernel(cells, advected, low, middle, high):
    rim = cells[:, 2 * R].reshape(L, 128).T
    for j in range(R):
        if j < H:
            ref, base = low, j
        elif j < R - H:
            ref, base = middle, j - H
        else:
            ref, base = high, j - (R - H)
        for h in range(2):
            tile = cells[:, h * R + j].reshape(L, 128).T
            ref[base, h * 128 : (h + 1) * 128, :] = tile
            advected[pl.ds(h * 128 * R + j, 128, stride=R), :] = tile
        ref[base, W:E, :] = rim[8 * j : 8 * j + 8]


def krylov_kernel(
    metric, vertical, inverses, south_inv, north_inv, south, low, middle, high, north,
    directions, images, sums, field, search,
):
    lane = lax.broadcasted_iota(jnp.int32, (1, L), 1)
    coef = vertical[...]
    upper_coef = jnp.where(lane == L - 1, 0.0, coef)
    lower_coef = jnp.where(lane == 0, 0.0, coef)

    def start(j):
        if j < 0:
            return south[j + H]
        if j < H:
            return low[j]
        if j < R - H:
            return middle[j - H]
        if j < R:
            return high[j - (R - H)]
        return north[j - R]

    def inverse(j):
        if j < 0:
            return south_inv[(j + H) * L : (j + H + 1) * L, :]
        if j >= R:
            return north_inv[(j - R) * L : (j - R + 1) * L, :]
        return inverses[j]

    def metric_of(j):
        if j < 0:
            return south_inv[H * L + j + H : H * L + j + H + 1, :]
        if j >= R:
            return north_inv[H * L + j - R : H * L + j - R + 1, :]
        return jnp.full((1, L), metric[j], jnp.float32)

    def precondition(j, value):
        m_high, m_low = halves(inverse(j))
        v_high, v_low = halves(value)
        right = jnp.concatenate(
            [
                jnp.concatenate([m_high, m_high], 1),
                jnp.concatenate([m_low, m_low], 1),
            ],
            0,
        )
        both = dot_nt(jnp.concatenate([v_high, v_low], 1), right)
        return both[:, :L] + both[:, L:]

    totals = [jnp.zeros((8, L), jnp.float32) for _ in range(9)]

    def add(index, a, b):
        totals[index] = totals[index] + jnp.sum((a * b).reshape(W // 8, 8, L), 0)

    for depth in range(3):
        reach = H - depth
        for j in range(-reach, R + reach):
            value = start(j) if depth == 0 else field[j + H]
            search[j + H] = precondition(j, value)
        for j in range(-reach + 1, R + reach - 1):
            q = search[j + H]
            m = metric_of(j)
            result = q * (2.0 * m + 2.0 * coef + 2.1)
            result = result - m * (pltpu.roll(q, 1, 0) + pltpu.roll(q, E - 1, 0))
            result = result - (search[j + H - 1] + search[j + H + 1])
            result = result - upper_coef * pltpu.roll(q, L - 1, 1)
            result = result - lower_coef * pltpu.roll(q, 1, 1)
            field[j + H] = result
            if 0 <= j < R:
                own = result[:W]
                directions[depth, j] = q[:W]
                images[depth, j] = own
                add(depth, start(j)[:W], own)
                for other in range(depth):
                    add(3 + depth * (depth + 1) // 2 + other, images[other, j], own)
                add(3 + depth * (depth + 1) // 2 + depth, own, own)
    row = jnp.zeros((1, L), jnp.float32)
    for index in range(9):
        total = jnp.sum(jnp.sum(totals[index], 0, keepdims=True), 1, keepdims=True)
        row = jnp.where(lane == index, total, row)
    sums[...] = jnp.broadcast_to(row, sums.shape)


def finish_kernel(sums, low, middle, high, directions, images, pressure, residual):
    lane = lax.broadcasted_iota(jnp.int32, (1, L), 1)
    row = jnp.sum(sums[...], 0, keepdims=True)

    def entry(index):
        value = jnp.sum(jnp.where(lane == index, row, 0.0), 1, keepdims=True)
        return jnp.broadcast_to(value, (1, L))

    b1, b2, b3, g11, g12, g22, g13, g23, g33 = (entry(i) for i in range(9))
    l21 = g12 / g11
    l31 = g13 / g11
    d2 = g22 - l21 * g12
    cross = g23 - l21 * g13
    l32 = cross / d2
    d3 = g33 - l31 * g13 - l32 * cross
    c2 = b2 - l21 * b1
    y1 = b1 / g11
    y2 = c2 / d2
    y3 = (b3 - l31 * b1 - l32 * c2) / d3
    k3 = y3
    k2 = y2 - l32 * k3
    k1 = y1 - l21 * k2 - l31 * k3
    for j in range(R):
        if j < H:
            first = low[j, :W]
        elif j < R - H:
            first = middle[j - H, :W]
        else:
            first = high[j - (R - H), :W]
        pressure[row_of(j), :] = (
            k1 * directions[0, j] + k2 * directions[1, j] + k3 * directions[2, j]
        )
        residual[row_of(j), :] = (
            first - k1 * images[0, j] - k2 * images[1, j] - k3 * images[2, j]
        )


VMEM = pl.BlockSpec(memory_space=pltpu.VMEM)
SMEM = pl.BlockSpec(memory_space=pltpu.SMEM)


def call(kernel, ins, outs, scratch=(), limit=32, cost=(0, 4 * MIB)):
    return pl.pallas_call(
        kernel,
        out_shape=tuple(jax.ShapeDtypeStruct(s, jnp.float32) for s in outs),
        in_specs=list(ins),
        out_specs=tuple(VMEM for _ in outs),
        scratch_shapes=[pltpu.VMEM(s, jnp.float32) for s in scratch],
        compiler_params=pltpu.CompilerParams(vmem_limit_bytes=limit * MIB),
        cost_estimate=pl.CostEstimate(
            flops=cost[0], bytes_accessed=cost[1], transcendentals=0
        ),
    )


def body(count, tracer, offsets, frac_lon, frac_lat, frac_lev, metric, vertical_coef, inverses):
    north_of = [(i, i + 1) for i in range(count - 1)]
    south_of = [(i + 1, i) for i in range(count - 1)]
    flat = tracer.reshape(W * R, L)
    up, down, up_inv, down_inv = call(
        edges_kernel,
        (VMEM, VMEM, SMEM),
        ((W, L), (2 * W, L), (H * L + 8, L), (H * L + 8, L)),
    )(flat, inverses, metric)
    south_row = lax.ppermute(up, LAT, north_of)
    north_rows = lax.ppermute(down, LAT, south_of)
    south_inv = lax.ppermute(up_inv, LAT, north_of)
    north_inv = lax.ppermute(down_inv, LAT, south_of)
    (turned,) = call(
        mix_kernel, (SMEM, SMEM, VMEM, VMEM, VMEM), ((NL, 2, R, 8, 128),)
    )(frac_lat, frac_lev, flat, south_row, north_rows)
    lines = lax.all_to_all(turned, LON, 0, 0, tiled=True)
    (moved,) = call(
        shift_kernel,
        (SMEM, SMEM, VMEM),
        ((NL, 2 * R + 1, 8, 128),),
        scratch=((2 * NL, R, 8, 128),),
    )(offsets, frac_lon, lines.reshape(2 * NL, R, 8, 128))
    back = lax.all_to_all(moved, LON, 0, 0, tiled=True)
    advected, low, middle, high = call(
        turn_kernel,
        (VMEM,),
        ((W * R, L), (H, E, L), (R - 2 * H, E, L), (H, E, L)),
    )(back)
    south = lax.ppermute(high, LAT, north_of)
    north = lax.ppermute(low, LAT, south_of)
    directions, images, sums = call(
        krylov_kernel,
        (SMEM,) + (VMEM,) * 9,
        ((3, R, W, L), (3, R, W, L), (count * NL, L)),
        scratch=((R + 2 * H, E, L), (R + 2 * H, E, L)),
    )(metric, vertical_coef.reshape(1, L), inverses, south_inv, north_inv, south, low, middle, high, north)
    gathered = lax.all_to_all(sums, LON_LAT, 0, 0, tiled=True)
    pressure, residual = call(
        finish_kernel, (VMEM,) * 6, ((W * R, L), (W * R, L))
    )(gathered, low, middle, high, directions, images)
    return tuple(x.reshape(W, R, L) for x in (advected, pressure, residual))


def solution(mesh):
    count = mesh.shape["lat"]
    split = Mesh(mesh.devices.reshape(4, 4, count // 2, 2), LON_LAT)
    placed = (P(LON, LAT, None), P(LAT), P(LAT), P(LAT), P(LAT), P(LAT), P(), P(LAT, None, None))
    return jax.shard_map(
        functools.partial(body, count),
        mesh=split,
        in_specs=placed,
        out_specs=(P(LON, LAT, None),) * 3,
        check_vma=False,
    )
```

```python
import functools

import jax
import jax.numpy as jnp
from jax import lax
from jax.experimental import pallas as pl
from jax.experimental.pallas import tpu as pltpu
from jax.sharding import Mesh
from jax.sharding import PartitionSpec as P

LON = ("lon_0", "lon_1")
LAT = ("lat_0", "lat_1")
LON_LAT = ("lon_0", "lon_1", "lat_0", "lat_1")
W = 256
R = 8
L = 128
H = 3
E = W + 8
NL = 16
B = 2 * NL
T = H * E
MIB = 1 << 20


def weights(f):
    sixth = 1.0 / 6.0
    return (
        -f * (f - 1.0) * (f - 2.0) * sixth,
        (f + 1.0) * (f - 1.0) * (f - 2.0) * 0.5,
        -(f + 1.0) * f * (f - 2.0) * 0.5,
        (f + 1.0) * f * (f - 1.0) * sixth,
    )


def halves(x):
    high = x.astype(jnp.bfloat16)
    return high, (x - high.astype(jnp.float32)).astype(jnp.bfloat16)


def dot_nt(a, b):
    return lax.dot_general(
        a, b, (((1,), (1,)), ((), ())), preferred_element_type=jnp.float32
    )


def row_of(j):
    return pl.ds(j, W, stride=R)


def is_even():
    return lax.axis_index("lat_1") == 0


def edges_kernel(tracer, pair, cross):
    even = is_even()
    last = tracer[row_of(R - 1), :]
    first = tracer[row_of(0), :]
    second = tracer[row_of(1), :]
    pair[0:W] = jnp.where(even, last, first)
    pair[W : 2 * W] = second
    cross[0:W] = jnp.where(even, first, last)
    cross[W : 2 * W] = second


def mix_kernel(fractions, tracer, pair, cross, out):
    even = is_even()
    delta = lax.broadcasted_iota(jnp.int32, (L, L), 1) - lax.broadcasted_iota(
        jnp.int32, (L, L), 0
    )

    def row(k):
        if k < 0:
            return jnp.where(even, cross[0:W], pair[0:W])
        if k >= R:
            part = slice((k - R) * W, (k - R + 1) * W)
            return jnp.where(even, pair[part], cross[part])
        return tracer[row_of(k), :]

    for j in range(R):
        w = weights(fractions[j : j + 1, :])
        mixed = w[0] * row(j - 1) + w[1] * row(j) + w[2] * row(j + 1) + w[3] * row(j + 2)
        v = weights(fractions[R + j : R + j + 1, :])
        table = jnp.zeros((L, L), jnp.float32)
        for m in range(4):
            table = jnp.where(delta == m - 1, v[m], table)
        t_high, t_low = halves(table)
        m_high, m_low = halves(mixed)
        left = jnp.concatenate(
            [
                jnp.concatenate([t_high, t_high], 1),
                jnp.concatenate([t_low, t_low], 1),
            ],
            0,
        )
        both = dot_nt(left, jnp.concatenate([m_high, m_low], 1))
        turned = (both[:L] + both[L:]).reshape(NL, 8, W)
        out[:, 0, j] = turned[:, :, :128]
        out[:, 1, j] = turned[:, :, 128:]


def shift_kernel(offsets, frac_lon, cells, out, twice):
    delta = lax.broadcasted_iota(jnp.int32, (128, 128), 0) - lax.broadcasted_iota(
        jnp.int32, (128, 128), 1
    )
    lane = lax.broadcasted_iota(jnp.int32, (1, 1, 128), 2)
    rims = jnp.zeros((NL, 8, 128), jnp.float32)
    for j in range(R):
        w = weights(frac_lon[j])
        off = offsets[j]
        turns = lax.shift_right_logical(off, 7)
        rest = jnp.bitwise_and(off, 127)
        placed = delta + rest
        left, right_high, right_low = [], [], []
        for k in range(3):
            table = jnp.zeros((128, 128), jnp.float32)
            for m in range(4):
                table = jnp.where(placed == m - 1 - 128 * (k - 1), w[m], table)
            t_high, t_low = halves(table)
            right_high += [t_high, t_high]
            right_low += [t_low, t_low]
            if k == 0:
                part = jnp.concatenate([cells[B - 1 :, j], cells[: B - 1, j]], 0)
            elif k == 1:
                part = cells[:, j]
            else:
                part = jnp.concatenate([cells[1:, j], cells[:1, j]], 0)
            left += list(halves(part.reshape(B * 8, 128)))
        right = jnp.concatenate(
            [jnp.concatenate(right_high, 0), jnp.concatenate(right_low, 0)], 1
        )
        both = jnp.dot(
            jnp.concatenate(left, 1), right, preferred_element_type=jnp.float32
        )
        value = (both[:, :128] + both[:, 128:]).reshape(B, 8, 128)
        twice[j, :B] = value
        twice[j, B:] = value
        start = jnp.bitwise_and(B - turns, B - 1)
        moved = twice[j, pl.ds(start, B)].reshape(NL, 2, 8, 128)
        near, far = moved[:, 0], moved[:, 1]
        out[:, j] = near
        out[:, R + j] = far
        east = jnp.concatenate([near[1:], near[:1]], 0)
        west = jnp.concatenate([far[NL - 1 :], far[: NL - 1]], 0)
        rim = jnp.where(lane < 64, east, west)
        if j > 0:
            rim = pltpu.roll(rim, 8 * j, 2)
        rims = jnp.where(jnp.bitwise_and(lane + (4 - 8 * j), 127) < 8, rim, rims)
    out[:, 2 * R] = rims


def turn_kernel(metric, inverses, cells, advected, ring, pair, cross):
    even = is_even()
    rim = cells[:, 2 * R].reshape(L, 128).T
    sub = lax.broadcasted_iota(jnp.int32, (8, L), 0)
    for j in range(R):
        for h in range(2):
            tile = cells[:, h * R + j].reshape(L, 128).T
            ring[j, h * 128 : (h + 1) * 128, :] = tile
            advected[pl.ds(h * 128 * R + j, 128, stride=R), :] = tile
        before = (8 * j - 8) % 128
        tail = jnp.where(sub < 4, rim[8 * j : 8 * j + 8], rim[before : before + 8])
        ring[j, W:E, :] = jnp.where(sub == 3, metric[j], tail)
    for i in range(H):
        for base, size, high, low in (
            (i * E, E, ring[R - H + i], ring[i]),
            (T + i * L, L, inverses[R - H + i], inverses[i]),
        ):
            pair[base : base + size] = jnp.where(even, high, low)
            cross[base : base + size] = jnp.where(even, low, high)


def vertical_rows(vertical):
    lane = lax.broadcasted_iota(jnp.int32, (1, L), 1)
    coef = vertical[...]
    return coef, jnp.where(lane == L - 1, 0.0, coef), jnp.where(lane == 0, 0.0, coef)


def precondition(inverse, value):
    m_high, m_low = halves(inverse)
    v_high, v_low = halves(value)
    right = jnp.concatenate(
        [
            jnp.concatenate([m_high, m_high], 1),
            jnp.concatenate([m_low, m_low], 1),
        ],
        0,
    )
    both = dot_nt(jnp.concatenate([v_high, v_low], 1), right)
    return both[:, :L] + both[:, L:]


def operate(q, south, north, m, rows):
    coef, upper, lower = rows
    result = q * (2.0 * m + 2.0 * coef + 2.1)
    result = result - m * (pltpu.roll(q, 1, 0) + pltpu.roll(q, E - 1, 0))
    result = result - (south + north)
    result = result - upper * pltpu.roll(q, L - 1, 1)
    return result - lower * pltpu.roll(q, 1, 1)


def partial(a, b):
    return jnp.sum((a[:W] * b[:W]).reshape(W // 8, 8, L), 0)


def gram(depth, other):
    return 3 + depth * (depth + 1) // 2 + other


def inside(depth, j):
    return depth < j < R - 1 - depth


def inner_kernel(metric, vertical, inverses, ring, search, field, totals):
    rows = vertical_rows(vertical)
    sums = [jnp.zeros((8, L), jnp.float32) for _ in range(9)]
    for depth in range(3):
        for j in range(depth, R - depth):
            search[depth, j] = precondition(
                inverses[j], ring[j] if depth == 0 else field[depth - 1, j]
            )
        for j in range(depth + 1, R - 1 - depth):
            result = operate(
                search[depth, j], search[depth, j - 1], search[depth, j + 1],
                jnp.full((1, L), metric[j], jnp.float32), rows,
            )
            field[depth, j] = result
            sums[depth] = sums[depth] + partial(ring[j], result)
            for other in range(depth):
                k = gram(depth, other)
                sums[k] = sums[k] + partial(field[other, j], result)
            k = gram(depth, depth)
            sums[k] = sums[k] + partial(result, result)
    for k in range(9):
        totals[k] = sums[k]


def outer_kernel(
    metric, vertical, inverses, ring, pair, cross, search, field, totals,
    new_search, new_field, sums_out, wide,
):
    even = is_even()
    lane = lax.broadcasted_iota(jnp.int32, (1, L), 1)
    rows = vertical_rows(vertical)
    sums = [totals[k] for k in range(9)]

    def beyond(j, base, size):
        part = slice(base, base + size)
        first, second = (cross, pair) if j < 0 else (pair, cross)
        return jnp.where(even, first[part], second[part])

    def inverse(j):
        if 0 <= j < R:
            return inverses[j]
        return beyond(j, T + (j + H if j < 0 else j - R) * L, L)

    def metric_of(j):
        if 0 <= j < R:
            return jnp.full((1, L), metric[j], jnp.float32)
        return beyond(j, (j + H if j < 0 else j - R) * E + W + 3, 1)

    def start(j):
        if 0 <= j < R:
            return ring[j]
        return beyond(j, (j + H if j < 0 else j - R) * E, E)

    def image(depth, j):
        if inside(depth, j):
            return field[depth, j]
        if 0 <= j < R:
            return new_field[depth, j]
        return wide[1, depth, j + H if j < 0 else j - R + H]

    def direction(depth, j):
        if depth <= j < R - depth:
            return search[depth, j]
        if 0 <= j < R:
            return new_search[depth, j]
        return wide[0, depth, j + H if j < 0 else j - R + H]

    for depth in range(3):
        reach = H - depth
        for j in range(-reach, R + reach):
            if depth <= j < R - depth:
                continue
            value = precondition(
                inverse(j), start(j) if depth == 0 else image(depth - 1, j)
            )
            if 0 <= j < R:
                new_search[depth, j] = value
            else:
                wide[0, depth, j + H if j < 0 else j - R + H] = value
        for j in range(-reach + 1, R + reach - 1):
            if inside(depth, j):
                continue
            result = operate(
                direction(depth, j), direction(depth, j - 1), direction(depth, j + 1),
                metric_of(j), rows,
            )
            if not 0 <= j < R:
                wide[1, depth, j + H if j < 0 else j - R + H] = result
                continue
            new_field[depth, j] = result
            sums[depth] = sums[depth] + partial(start(j), result)
            for other in range(depth):
                k = gram(depth, other)
                sums[k] = sums[k] + partial(image(other, j), result)
            k = gram(depth, depth)
            sums[k] = sums[k] + partial(result, result)
    row = jnp.zeros((1, L), jnp.float32)
    for k in range(9):
        total = jnp.sum(jnp.sum(sums[k], 0, keepdims=True), 1, keepdims=True)
        row = jnp.where(lane == k, total, row)
    sums_out[...] = jnp.broadcast_to(row, sums_out.shape)


def finish_kernel(
    sums, ring, search, field, new_search, new_field, pressure, residual, held, left, sems
):
    lane = lax.broadcasted_iota(jnp.int32, (1, L), 1)
    row = jnp.sum(sums[...], 0, keepdims=True)

    def entry(index):
        value = jnp.sum(jnp.where(lane == index, row, 0.0), 1, keepdims=True)
        return jnp.broadcast_to(value, (1, L))

    b1, b2, b3, g11, g12, g22, g13, g23, g33 = (entry(i) for i in range(9))
    l21 = g12 / g11
    l31 = g13 / g11
    d2 = g22 - l21 * g12
    cross = g23 - l21 * g13
    l32 = cross / d2
    d3 = g33 - l31 * g13 - l32 * cross
    c2 = b2 - l21 * b1
    y1 = b1 / g11
    y2 = c2 / d2
    y3 = (b3 - l31 * b1 - l32 * c2) / d3
    k3 = y3
    k2 = y2 - l32 * k3
    k1 = y1 - l21 * k2 - l31 * k3
    parts = 4
    size = W // parts
    copies = []
    for part in range(parts):
        span = slice(part * size, (part + 1) * size)
        for j in range(R):
            q = [
                (search if depth <= j < R - depth else new_search)[depth, j, span]
                for depth in range(3)
            ]
            v = [
                (field if inside(depth, j) else new_field)[depth, j, span]
                for depth in range(3)
            ]
            to = pl.ds(part * size * R + j, size, stride=R)
            held[to, :] = k1 * q[0] + k2 * q[1] + k3 * q[2]
            left[to, :] = ring[j, span] - k1 * v[0] - k2 * v[1] - k3 * v[2]
        block = pl.ds(part * size * R, size * R)
        for i, (source, target) in enumerate(((held, pressure), (left, residual))):
            copy = pltpu.make_async_copy(
                source.at[block, :], target.at[block, :], sems.at[part, i]
            )
            copy.start()
            copies.append(copy)
    for copy in copies:
        copy.wait()


VMEM = pl.BlockSpec(memory_space=pltpu.VMEM)
SMEM = pl.BlockSpec(memory_space=pltpu.SMEM)
HBM = pl.BlockSpec(memory_space=pltpu.HBM)


def call(kernel, ins, outs, scratch=(), limit=32, flops=0, where=VMEM):
    return pl.pallas_call(
        kernel,
        out_shape=tuple(jax.ShapeDtypeStruct(s, jnp.float32) for s in outs),
        in_specs=list(ins),
        out_specs=tuple(where for _ in outs),
        scratch_shapes=[
            pltpu.VMEM(s, jnp.float32) if isinstance(s, tuple) else s for s in scratch
        ],
        compiler_params=pltpu.CompilerParams(vmem_limit_bytes=limit * MIB),
        cost_estimate=pl.CostEstimate(
            flops=flops, bytes_accessed=8 * MIB, transcendentals=0
        ),
    )


def body(count, tracer, offsets, frac_lon, frac_lat, frac_lev, metric, vertical_coef, inverses):
    in_chip = [(i, i ^ 1) for i in range(count)]
    across = [(i, i - 1 + 2 * (i % 2)) for i in range(1, count - 1)]
    flat = tracer.reshape(W * R, L)
    pair_out, cross_out = call(edges_kernel, (VMEM,), ((2 * W, L), (2 * W, L)))(flat)
    cross_in = lax.ppermute(cross_out, LAT, across)
    pair_in = lax.ppermute(pair_out, LAT, in_chip)
    fractions = jnp.broadcast_to(
        jnp.concatenate([frac_lat, frac_lev])[:, None], (2 * R, L)
    )
    (turned,) = call(mix_kernel, (VMEM,) * 4, ((NL, 2, R, 8, 128),))(
        fractions, flat, pair_in, cross_in
    )
    lines = lax.all_to_all(turned, LON, 0, 0, tiled=True)
    (moved,) = call(
        shift_kernel,
        (SMEM, SMEM, VMEM),
        ((NL, 2 * R + 1, 8, 128),),
        scratch=((R, 2 * B, 8, 128),),
    )(offsets, frac_lon, lines.reshape(B, R, 8, 128))
    back = lax.all_to_all(moved, LON, 0, 0, tiled=True)
    advected, ring, pair_out, cross_out = call(
        turn_kernel,
        (SMEM, VMEM, VMEM),
        ((W * R, L), (R, E, L), (T + H * L, L), (T + H * L, L)),
    )(metric, inverses, back)
    cross = lax.ppermute(cross_out, LAT, across)
    pair = lax.ppermute(pair_out, LAT, in_chip)
    vertical = vertical_coef.reshape(1, L)
    search, images, totals = call(
        inner_kernel,
        (SMEM, VMEM, VMEM, VMEM),
        ((3, R, E, L), (3, R, E, L), (9, 8, L)),
        flops=2 * 10**9,
    )(metric, vertical, inverses, ring)
    new_search, new_images, sums = call(
        outer_kernel,
        (SMEM,) + (VMEM,) * 8,
        ((3, R, E, L), (3, R, E, L), (count * NL, L)),
        scratch=((2, 3, 2 * H, E, L),),
    )(metric, vertical, inverses, ring, pair, cross, search, images, totals)
    gathered = lax.all_to_all(sums, LON_LAT, 0, 0, tiled=True)
    pressure, residual = call(
        finish_kernel,
        (VMEM,) * 6,
        ((W * R, L), (W * R, L)),
        scratch=((W * R, L), (W * R, L), pltpu.SemaphoreType.DMA((4, 2))),
        where=HBM,
    )(gathered, ring, search, images, new_search, new_images)
    return tuple(x.reshape(W, R, L) for x in (advected, pressure, residual))


def solution(mesh):
    count = mesh.shape["lat"]
    split = Mesh(mesh.devices.reshape(4, 4, count // 2, 2), LON_LAT)
    placed = (P(LON, LAT, None), P(LAT), P(LAT), P(LAT), P(LAT), P(LAT), P(), P(LAT, None, None))
    return jax.shard_map(
        functools.partial(body, count),
        mesh=split,
        in_specs=placed,
        out_specs=(P(LON, LAT, None),) * 3,
        check_vma=False,
    )
```

```python
import functools

import jax
import jax.numpy as jnp
from jax import lax
from jax.experimental import pallas as pl
from jax.experimental.pallas import tpu as pltpu
from jax.sharding import Mesh
from jax.sharding import PartitionSpec as P

LON = ("lon_0", "lon_1")
LAT = ("lat_0", "lat_1")
LON_LAT = ("lon_0", "lon_1", "lat_0", "lat_1")
W = 256
R = 8
L = 128
H = 3
E = W + 8
NL = 16
B = 2 * NL
T = H * E
MIB = 1 << 20


def weights(f):
    sixth = 1.0 / 6.0
    return (
        -f * (f - 1.0) * (f - 2.0) * sixth,
        (f + 1.0) * (f - 1.0) * (f - 2.0) * 0.5,
        -(f + 1.0) * f * (f - 2.0) * 0.5,
        (f + 1.0) * f * (f - 1.0) * sixth,
    )


def halves(x):
    high = x.astype(jnp.bfloat16)
    return high, (x - high.astype(jnp.float32)).astype(jnp.bfloat16)


def dot_nt(a, b):
    return lax.dot_general(
        a, b, (((1,), (1,)), ((), ())), preferred_element_type=jnp.float32
    )


def row_of(j):
    return pl.ds(j, W, stride=R)


def is_even():
    return lax.axis_index("lat_1") == 0


def at_end():
    place = 2 * lax.axis_index("lat_0") + lax.axis_index("lat_1")
    return (place == 0) | (place == 2 * lax.axis_size("lat_0") - 1)


def edges_kernel(tracer, pair, cross):
    even, end = is_even(), at_end()
    last = tracer[row_of(R - 1), :]
    first = tracer[row_of(0), :]
    second = tracer[row_of(1), :]
    pair[0:W] = jnp.where(even, last, first)
    pair[W : 2 * W] = second
    cross[0:W] = jnp.where(end, 0.0, jnp.where(even, first, last))
    cross[W : 2 * W] = jnp.where(end, 0.0, second)


def mix_kernel(fractions, tracer, pair, cross, out):
    even = is_even()
    delta = lax.broadcasted_iota(jnp.int32, (L, L), 1) - lax.broadcasted_iota(
        jnp.int32, (L, L), 0
    )

    def row(k):
        if k < 0:
            return jnp.where(even, cross[0:W], pair[0:W])
        if k >= R:
            part = slice((k - R) * W, (k - R + 1) * W)
            return jnp.where(even, pair[part], cross[part])
        return tracer[row_of(k), :]

    for j in range(R):
        w = weights(fractions[j : j + 1, :])
        mixed = w[0] * row(j - 1) + w[1] * row(j) + w[2] * row(j + 1) + w[3] * row(j + 2)
        v = weights(fractions[R + j : R + j + 1, :])
        table = jnp.zeros((L, L), jnp.float32)
        for m in range(4):
            table = jnp.where(delta == m - 1, v[m], table)
        t_high, t_low = halves(table)
        m_high, m_low = halves(mixed)
        left = jnp.concatenate(
            [
                jnp.concatenate([t_high, t_high], 1),
                jnp.concatenate([t_low, t_low], 1),
            ],
            0,
        )
        both = dot_nt(left, jnp.concatenate([m_high, m_low], 1))
        turned = (both[:L] + both[L:]).reshape(NL, 8, W)
        out[:, 0, j] = turned[:, :, :128]
        out[:, 1, j] = turned[:, :, 128:]


def shift_kernel(offsets, frac_lon, cells, arrived, out, twice):
    delta = lax.broadcasted_iota(jnp.int32, (128, 128), 0) - lax.broadcasted_iota(
        jnp.int32, (128, 128), 1
    )
    lane = lax.broadcasted_iota(jnp.int32, (1, 1, 128), 2)
    rims = jnp.zeros((NL, 8, 128), jnp.float32)
    for j in range(R):
        w = weights(frac_lon[j])
        off = offsets[j]
        turns = lax.shift_right_logical(off, 7)
        rest = jnp.bitwise_and(off, 127)
        placed = delta + rest
        left, right_high, right_low = [], [], []
        for k in range(3):
            table = jnp.zeros((128, 128), jnp.float32)
            for m in range(4):
                table = jnp.where(placed == m - 1 - 128 * (k - 1), w[m], table)
            t_high, t_low = halves(table)
            right_high += [t_high, t_high]
            right_low += [t_low, t_low]
            if k == 0:
                part = jnp.concatenate([cells[B - 1 :, j], cells[: B - 1, j]], 0)
            elif k == 1:
                part = cells[:, j]
            else:
                part = jnp.concatenate([cells[1:, j], cells[:1, j]], 0)
            left += list(halves(part.reshape(B * 8, 128)))
        right = jnp.concatenate(
            [jnp.concatenate(right_high, 0), jnp.concatenate(right_low, 0)], 1
        )
        both = jnp.dot(
            jnp.concatenate(left, 1), right, preferred_element_type=jnp.float32
        )
        value = (both[:, :128] + both[:, 128:]).reshape(B, 8, 128)
        twice[j, :B] = value
        twice[j, B:] = value
        start = jnp.bitwise_and(B - turns, B - 1)
        moved = twice[j, pl.ds(start, B)].reshape(NL, 2, 8, 128)
        near, far = moved[:, 0], moved[:, 1]
        out[:, j] = near
        out[:, R + j] = far
        east = jnp.concatenate([near[1:], near[:1]], 0)
        west = jnp.concatenate([far[NL - 1 :], far[: NL - 1]], 0)
        rim = jnp.where(lane < 64, east, west)
        if j > 0:
            rim = pltpu.roll(rim, 8 * j, 2)
        rims = jnp.where(jnp.bitwise_and(lane + (4 - 8 * j), 127) < 8, rim, rims)
    out[:, 2 * R] = rims


def edge(j):
    return j < H or j >= R - H


def turned_row(cells, rim, metric, j, ref, at):
    sub = lax.broadcasted_iota(jnp.int32, (8, L), 0)
    for h in range(2):
        ref[at, h * 128 : (h + 1) * 128, :] = cells[:, h * R + j].reshape(L, 128).T
    before = (8 * j - 8) % 128
    tail = jnp.where(sub < 4, rim[8 * j : 8 * j + 8], rim[before : before + 8])
    ref[at, W:E, :] = jnp.where(sub == 3, metric[j], tail)


def turn_kernel(metric, inverses, cells, ring, pair, cross):
    even, end = is_even(), at_end()
    rim = cells[:, 2 * R].reshape(L, 128).T
    for j in range(R):
        if edge(j):
            turned_row(cells, rim, metric, j, ring, j)
    for i in range(H):
        high, low = ring[R - H + i], ring[i]
        pair[i * E : (i + 1) * E] = jnp.where(even, high, low)
        cross[i * E : (i + 1) * E] = jnp.where(end, 0.0, jnp.where(even, low, high))
        pair[T + i * L : T + (i + 1) * L] = jnp.where(even, inverses[R - H + i], inverses[i])


def vertical_rows(vertical):
    lane = lax.broadcasted_iota(jnp.int32, (1, L), 1)
    coef = vertical[...]
    return coef, jnp.where(lane == L - 1, 0.0, coef), jnp.where(lane == 0, 0.0, coef)


def precondition(inverse, value):
    m_high, m_low = halves(inverse)
    v_high, v_low = halves(value)
    right = jnp.concatenate(
        [
            jnp.concatenate([m_high, m_high], 1),
            jnp.concatenate([m_low, m_low], 1),
        ],
        0,
    )
    both = dot_nt(jnp.concatenate([v_high, v_low], 1), right)
    return both[:, :L] + both[:, L:]


def operate(q, south, north, m, rows):
    coef, upper, lower = rows
    result = q * (2.0 * m + 2.0 * coef + 2.1)
    result = result - m * (pltpu.roll(q, 1, 0) + pltpu.roll(q, E - 1, 0))
    result = result - (south + north)
    result = result - upper * pltpu.roll(q, L - 1, 1)
    return result - lower * pltpu.roll(q, 1, 1)


def partial(a, b):
    return jnp.sum((a[:W] * b[:W]).reshape(W // 8, 8, L), 0)


def gram(depth, other):
    return 3 + depth * (depth + 1) // 2 + other


def inside(depth, j):
    return depth < j < R - 1 - depth


def inner_kernel(
    metric, vertical, inverses, cells, edges, search, field, totals, middle, advected, ring
):
    rim = cells[:, 2 * R].reshape(L, 128).T
    for j in range(R):
        if edge(j):
            ring[j] = edges[j]
        else:
            turned_row(cells, rim, metric, j, ring, j)
            middle[j - H] = ring[j]
        advected[row_of(j), :] = ring[j, :W]
    rows = vertical_rows(vertical)
    sums = [jnp.zeros((8, L), jnp.float32) for _ in range(9)]
    for depth in range(3):
        for j in range(depth, R - depth):
            search[depth, j] = precondition(
                inverses[j], ring[j] if depth == 0 else field[depth - 1, j]
            )
        for j in range(depth + 1, R - 1 - depth):
            result = operate(
                search[depth, j], search[depth, j - 1], search[depth, j + 1],
                jnp.full((1, L), metric[j], jnp.float32), rows,
            )
            field[depth, j] = result
            sums[depth] = sums[depth] + partial(ring[j], result)
            for other in range(depth):
                k = gram(depth, other)
                sums[k] = sums[k] + partial(field[other, j], result)
            k = gram(depth, depth)
            sums[k] = sums[k] + partial(result, result)
    for k in range(9):
        totals[k] = sums[k]


def outer_kernel(
    metric, vertical, inverses, cross_inv, edges, middle, pair, cross, search, field, totals,
    new_search, new_field, sums_out, wide,
):
    even = is_even()
    lane = lax.broadcasted_iota(jnp.int32, (1, L), 1)
    rows = vertical_rows(vertical)
    sums = [totals[k] for k in range(9)]

    def beyond(j, base, size):
        part = slice(base, base + size)
        first, second = (cross, pair) if j < 0 else (pair, cross)
        return jnp.where(even, first[part], second[part])

    def inverse(j):
        if 0 <= j < R:
            return inverses[j]
        i = j + H if j < 0 else j - R
        near = pair[T + i * L : T + (i + 1) * L]
        far = cross_inv[i * L : (i + 1) * L]
        return jnp.where(even, far, near) if j < 0 else jnp.where(even, near, far)

    def metric_of(j):
        if 0 <= j < R:
            return jnp.full((1, L), metric[j], jnp.float32)
        return beyond(j, (j + H if j < 0 else j - R) * E + W + 3, 1)

    def start(j):
        if 0 <= j < R:
            return edges[j] if edge(j) else middle[j - H]
        return beyond(j, (j + H if j < 0 else j - R) * E, E)

    def image(depth, j):
        if inside(depth, j):
            return field[depth, j]
        if 0 <= j < R:
            return new_field[depth, j]
        return wide[1, depth, j + H if j < 0 else j - R + H]

    def direction(depth, j):
        if depth <= j < R - depth:
            return search[depth, j]
        if 0 <= j < R:
            return new_search[depth, j]
        return wide[0, depth, j + H if j < 0 else j - R + H]

    for depth in range(3):
        reach = H - depth
        for j in range(-reach, R + reach):
            if depth <= j < R - depth:
                continue
            value = precondition(
                inverse(j), start(j) if depth == 0 else image(depth - 1, j)
            )
            if 0 <= j < R:
                new_search[depth, j] = value
            else:
                wide[0, depth, j + H if j < 0 else j - R + H] = value
        for j in range(-reach + 1, R + reach - 1):
            if inside(depth, j):
                continue
            result = operate(
                direction(depth, j), direction(depth, j - 1), direction(depth, j + 1),
                metric_of(j), rows,
            )
            if not 0 <= j < R:
                wide[1, depth, j + H if j < 0 else j - R + H] = result
                continue
            new_field[depth, j] = result
            sums[depth] = sums[depth] + partial(start(j), result)
            for other in range(depth):
                k = gram(depth, other)
                sums[k] = sums[k] + partial(image(other, j), result)
            k = gram(depth, depth)
            sums[k] = sums[k] + partial(result, result)
    row = jnp.zeros((1, L), jnp.float32)
    for k in range(9):
        total = jnp.sum(jnp.sum(sums[k], 0, keepdims=True), 1, keepdims=True)
        row = jnp.where(lane == k, total, row)
    sums_out[...] = jnp.broadcast_to(row, sums_out.shape)


def finish_kernel(
    sums, edges, middle, search, field, new_search, new_field, pressure, residual, held, left, sems
):
    lane = lax.broadcasted_iota(jnp.int32, (1, L), 1)
    row = jnp.sum(sums[...], 0, keepdims=True)

    def entry(index):
        value = jnp.sum(jnp.where(lane == index, row, 0.0), 1, keepdims=True)
        return jnp.broadcast_to(value, (1, L))

    b1, b2, b3, g11, g12, g22, g13, g23, g33 = (entry(i) for i in range(9))
    l21 = g12 / g11
    l31 = g13 / g11
    d2 = g22 - l21 * g12
    cross = g23 - l21 * g13
    l32 = cross / d2
    d3 = g33 - l31 * g13 - l32 * cross
    c2 = b2 - l21 * b1
    y1 = b1 / g11
    y2 = c2 / d2
    y3 = (b3 - l31 * b1 - l32 * c2) / d3
    k3 = y3
    k2 = y2 - l32 * k3
    k1 = y1 - l21 * k2 - l31 * k3
    parts = 4
    size = W // parts
    copies = []
    for part in range(parts):
        span = slice(part * size, (part + 1) * size)
        for j in range(R):
            q = [
                (search if depth <= j < R - depth else new_search)[depth, j, span]
                for depth in range(3)
            ]
            v = [
                (field if inside(depth, j) else new_field)[depth, j, span]
                for depth in range(3)
            ]
            to = pl.ds(part * size * R + j, size, stride=R)
            held[to, :] = k1 * q[0] + k2 * q[1] + k3 * q[2]
            first = edges[j, span] if edge(j) else middle[j - H, span]
            left[to, :] = first - k1 * v[0] - k2 * v[1] - k3 * v[2]
        block = pl.ds(part * size * R, size * R)
        for i, (source, target) in enumerate(((held, pressure), (left, residual))):
            copy = pltpu.make_async_copy(
                source.at[block, :], target.at[block, :], sems.at[part, i]
            )
            copy.start()
            copies.append(copy)
    for copy in copies:
        copy.wait()


VMEM = pl.BlockSpec(memory_space=pltpu.VMEM)
SMEM = pl.BlockSpec(memory_space=pltpu.SMEM)
HBM = pl.BlockSpec(memory_space=pltpu.HBM)
ANY = pl.BlockSpec(memory_space=pl.ANY)


def call(kernel, ins, outs, scratch=(), limit=32, flops=0, where=VMEM):
    return pl.pallas_call(
        kernel,
        out_shape=tuple(jax.ShapeDtypeStruct(s, jnp.float32) for s in outs),
        in_specs=list(ins),
        out_specs=tuple(where for _ in outs),
        scratch_shapes=[
            pltpu.VMEM(s, jnp.float32) if isinstance(s, tuple) else s for s in scratch
        ],
        compiler_params=pltpu.CompilerParams(vmem_limit_bytes=limit * MIB),
        cost_estimate=pl.CostEstimate(
            flops=flops, bytes_accessed=8 * MIB, transcendentals=0
        ),
    )


def body(count, tracer, offsets, frac_lon, frac_lat, frac_lev, metric, vertical_coef, inverses):
    in_chip = [(i, i ^ 1) for i in range(count)]
    across = [(i, (i - 1 + 2 * (i % 2)) % count) for i in range(count)]
    flat = tracer.reshape(W * R, L)
    pair_out, cross_out = call(edges_kernel, (VMEM,), ((2 * W, L), (2 * W, L)))(flat)
    cross_in = lax.ppermute(cross_out, LAT, across)
    pair_in = lax.ppermute(pair_out, LAT, in_chip)
    fractions = jnp.broadcast_to(
        jnp.concatenate([frac_lat, frac_lev])[:, None], (2 * R, L)
    )
    (turned,) = call(mix_kernel, (VMEM,) * 4, ((NL, 2, R, 8, 128),))(
        fractions, flat, pair_in, cross_in
    )
    first = jnp.where(is_even(), 0, R - H)
    inv_out = lax.dynamic_slice_in_dim(inverses, first, H, 0).reshape(H * L, L)
    inv_out = jnp.where(at_end(), 0.0, inv_out)
    inv_in = lax.ppermute(inv_out, LAT, across)
    lines = lax.all_to_all(turned, LON, 0, 0, tiled=True)
    (moved,) = call(
        shift_kernel,
        (SMEM, SMEM, VMEM, ANY),
        ((NL, 2 * R + 1, 8, 128),),
        scratch=((R, 2 * B, 8, 128),),
    )(offsets, frac_lon, lines.reshape(B, R, 8, 128), inv_in)
    back = lax.all_to_all(moved, LON, 0, 0, tiled=True)
    edges, pair_out, cross_out = call(
        turn_kernel, (SMEM, VMEM, VMEM), ((R, E, L), (T + H * L, L), (T, L))
    )(metric, inverses, back)
    cross = lax.ppermute(cross_out, LAT, across)
    pair = lax.ppermute(pair_out, LAT, in_chip)
    vertical = vertical_coef.reshape(1, L)
    search, images, totals, middle, advected = call(
        inner_kernel,
        (SMEM, VMEM, VMEM, VMEM, VMEM),
        ((3, R, E, L), (3, R, E, L), (9, 8, L), (R - 2 * H, E, L), (W * R, L)),
        scratch=((R, E, L),),
        flops=2 * 10**9,
    )(metric, vertical, inverses, back, edges)
    new_search, new_images, sums = call(
        outer_kernel,
        (SMEM,) + (VMEM,) * 10,
        ((3, R, E, L), (3, R, E, L), (count * NL, L)),
        scratch=((2, 3, 2 * H, E, L),),
    )(metric, vertical, inverses, inv_in, edges, middle, pair, cross, search, images, totals)
    gathered = lax.all_to_all(sums, LON_LAT, 0, 0, tiled=True)
    pressure, residual = call(
        finish_kernel,
        (VMEM,) * 7,
        ((W * R, L), (W * R, L)),
        scratch=((W * R, L), (W * R, L), pltpu.SemaphoreType.DMA((4, 2))),
        where=HBM,
    )(gathered, edges, middle, search, images, new_search, new_images)
    return tuple(x.reshape(W, R, L) for x in (advected, pressure, residual))


def solution(mesh):
    count = mesh.shape["lat"]
    split = Mesh(mesh.devices.reshape(4, 4, count // 2, 2), LON_LAT)
    placed = (P(LON, LAT, None), P(LAT), P(LAT), P(LAT), P(LAT), P(LAT), P(), P(LAT, None, None))
    return jax.shard_map(
        functools.partial(body, count),
        mesh=split,
        in_specs=placed,
        out_specs=(P(LON, LAT, None),) * 3,
        check_vma=False,
    )
```

```python
import functools

import jax
import jax.numpy as jnp
from jax import lax
from jax.experimental import pallas as pl
from jax.experimental.pallas import tpu as pltpu
from jax.sharding import Mesh
from jax.sharding import PartitionSpec as P

LON = ("lon_0", "lon_1")
LAT = ("lat_0", "lat_1")
LON_LAT = ("lon_0", "lon_1", "lat_0", "lat_1")
W = 256
R = 8
L = 128
H = 3
E = W + 8
NL = 16
B = 2 * NL
T = H * E
MIB = 1 << 20
CORE = (1, 2, 3, 4, 5)
SIDE = (0, 6, 7)


def weights(f):
    sixth = 1.0 / 6.0
    return (
        -f * (f - 1.0) * (f - 2.0) * sixth,
        (f + 1.0) * (f - 1.0) * (f - 2.0) * 0.5,
        -(f + 1.0) * f * (f - 2.0) * 0.5,
        (f + 1.0) * f * (f - 1.0) * sixth,
    )


def halves(x):
    high = x.astype(jnp.bfloat16)
    return high, (x - high.astype(jnp.float32)).astype(jnp.bfloat16)


def dot_nt(a, b):
    return lax.dot_general(
        a, b, (((1,), (1,)), ((), ())), preferred_element_type=jnp.float32
    )


def row_of(j):
    return pl.ds(j, W, stride=R)


def is_even():
    return lax.axis_index("lat_1") == 0


def at_end():
    place = 2 * lax.axis_index("lat_0") + lax.axis_index("lat_1")
    return (place == 0) | (place == 2 * lax.axis_size("lat_0") - 1)


def edges_kernel(tracer, pair, cross):
    even, end = is_even(), at_end()
    last = tracer[row_of(R - 1), :]
    first = tracer[row_of(0), :]
    second = tracer[row_of(1), :]
    pair[0:W] = jnp.where(even, last, first)
    pair[W : 2 * W] = second
    cross[0:W] = jnp.where(end, 0.0, jnp.where(even, first, last))
    cross[W : 2 * W] = jnp.where(end, 0.0, second)


def mix_rows(rows, row, fractions, held, out, sems):
    delta = lax.broadcasted_iota(jnp.int32, (L, L), 1) - lax.broadcasted_iota(
        jnp.int32, (L, L), 0
    )
    copies = []
    for at, j in enumerate(rows):
        w = weights(fractions[j : j + 1, :])
        mixed = w[0] * row(j - 1) + w[1] * row(j) + w[2] * row(j + 1) + w[3] * row(j + 2)
        v = weights(fractions[R + j : R + j + 1, :])
        table = jnp.zeros((L, L), jnp.float32)
        for m in range(4):
            table = jnp.where(delta == m - 1, v[m], table)
        t_high, t_low = halves(table)
        m_high, m_low = halves(mixed)
        left = jnp.concatenate(
            [
                jnp.concatenate([t_high, t_high], 1),
                jnp.concatenate([t_low, t_low], 1),
            ],
            0,
        )
        both = dot_nt(left, jnp.concatenate([m_high, m_low], 1))
        turned = (both[:L] + both[L:]).reshape(NL, 8, W)
        held[at, :, 0] = turned[:, :, :128]
        held[at, :, 1] = turned[:, :, 128:]
        copies.append(
            pltpu.make_async_copy(held.at[at], out.at[:, :, j], sems.at[at])
        )
        copies[-1].start()
    for copy in copies:
        copy.wait()


def mix_core_kernel(fractions, tracer, out, held, sems):
    mix_rows(CORE, lambda k: tracer[row_of(k), :], fractions, held, out, sems)


def mix_side_kernel(fractions, tracer, pair, cross, begun, out, held, sems):
    even = is_even()

    def row(k):
        if k < 0:
            return jnp.where(even, cross[0:W], pair[0:W])
        if k >= R:
            part = slice((k - R) * W, (k - R + 1) * W)
            return jnp.where(even, pair[part], cross[part])
        return tracer[row_of(k), :]

    mix_rows(SIDE, row, fractions, held, out, sems)


def shift_kernel(offsets, frac_lon, cells, out, twice):
    delta = lax.broadcasted_iota(jnp.int32, (128, 128), 0) - lax.broadcasted_iota(
        jnp.int32, (128, 128), 1
    )
    lane = lax.broadcasted_iota(jnp.int32, (1, 1, 128), 2)
    rims = jnp.zeros((NL, 8, 128), jnp.float32)
    for j in range(R):
        w = weights(frac_lon[j])
        off = offsets[j]
        turns = lax.shift_right_logical(off, 7)
        rest = jnp.bitwise_and(off, 127)
        placed = delta + rest
        left, right_high, right_low = [], [], []
        for k in range(3):
            table = jnp.zeros((128, 128), jnp.float32)
            for m in range(4):
                table = jnp.where(placed == m - 1 - 128 * (k - 1), w[m], table)
            t_high, t_low = halves(table)
            right_high += [t_high, t_high]
            right_low += [t_low, t_low]
            if k == 0:
                part = jnp.concatenate([cells[B - 1 :, j], cells[: B - 1, j]], 0)
            elif k == 1:
                part = cells[:, j]
            else:
                part = jnp.concatenate([cells[1:, j], cells[:1, j]], 0)
            left += list(halves(part.reshape(B * 8, 128)))
        right = jnp.concatenate(
            [jnp.concatenate(right_high, 0), jnp.concatenate(right_low, 0)], 1
        )
        both = jnp.dot(
            jnp.concatenate(left, 1), right, preferred_element_type=jnp.float32
        )
        value = (both[:, :128] + both[:, 128:]).reshape(B, 8, 128)
        twice[j, :B] = value
        twice[j, B:] = value
        start = jnp.bitwise_and(B - turns, B - 1)
        moved = twice[j, pl.ds(start, B)].reshape(NL, 2, 8, 128)
        near, far = moved[:, 0], moved[:, 1]
        out[:, j] = near
        out[:, R + j] = far
        east = jnp.concatenate([near[1:], near[:1]], 0)
        west = jnp.concatenate([far[NL - 1 :], far[: NL - 1]], 0)
        rim = jnp.where(lane < 64, east, west)
        if j > 0:
            rim = pltpu.roll(rim, 8 * j, 2)
        rims = jnp.where(jnp.bitwise_and(lane + (4 - 8 * j), 127) < 8, rim, rims)
    out[:, 2 * R] = rims


def edge(j):
    return j < H or j >= R - H


def turned_row(cells, rim, j, ref, at):
    sub = lax.broadcasted_iota(jnp.int32, (8, L), 0)
    for h in range(2):
        ref[at, h * 128 : (h + 1) * 128, :] = cells[:, h * R + j].reshape(L, 128).T
    before = (8 * j - 8) % 128
    tail = jnp.where(sub < 4, rim[8 * j : 8 * j + 8], rim[before : before + 8])
    ref[at, W:E, :] = tail


def vertical_rows(vertical):
    lane = lax.broadcasted_iota(jnp.int32, (1, L), 1)
    coef = vertical[...]
    return coef, jnp.where(lane == L - 1, 0.0, coef), jnp.where(lane == 0, 0.0, coef)


def precondition(inverse, value):
    m_high, m_low = halves(inverse)
    v_high, v_low = halves(value)
    right = jnp.concatenate(
        [
            jnp.concatenate([m_high, m_high], 1),
            jnp.concatenate([m_low, m_low], 1),
        ],
        0,
    )
    both = dot_nt(jnp.concatenate([v_high, v_low], 1), right)
    return both[:, :L] + both[:, L:]


def alone(q, m, rows):
    coef, upper, lower = rows
    result = q * (2.0 * m + 2.0 * coef + 2.1)
    result = result - m * (pltpu.roll(q, 1, 0) + pltpu.roll(q, E - 1, 0))
    result = result - upper * pltpu.roll(q, L - 1, 1)
    return result - lower * pltpu.roll(q, 1, 1)


def operate(q, south, north, m, rows):
    return alone(q, m, rows) - (south + north)


def metric_row(metric, j):
    return jnp.full((1, L), metric[j], jnp.float32)


Q1 = {0: 0, 1: 1, 2: 2, 5: 3, 6: 4, 7: 5}
V1_PART = {0: 6, 7: 7}
V1 = {1: 8, 6: 9}
Q2_PART = {0: 10, 7: 11}
Q2 = {1: 12, 6: 13}
V2_PART = {0: 14, 7: 15}
EARLY = 16
ENDS = ((0, 1, 2, 3), (7, 6, 5, 4))


def turn_kernel(metric, vertical, inverses, cells, ring, pair, cross, early):
    even, end = is_even(), at_end()
    rows = vertical_rows(vertical)
    rim = cells[:, 2 * R].reshape(L, 128).T
    for j in range(R):
        if edge(j):
            turned_row(cells, rim, j, ring, j)
            early[Q1[j]] = precondition(inverses[j], ring[j])
    for e, i, i2, _ in ENDS:
        early[V1_PART[e]] = alone(early[Q1[e]], metric_row(metric, e), rows) - early[Q1[i]]
        early[V1[i]] = operate(
            early[Q1[i]], early[Q1[e]], early[Q1[i2]], metric_row(metric, i), rows
        )
    for e, i, _, _ in ENDS:
        early[Q2_PART[e]] = precondition(inverses[e], early[V1_PART[e]])
        early[Q2[i]] = precondition(inverses[i], early[V1[i]])
    for e, i, _, _ in ENDS:
        early[V2_PART[e]] = (
            alone(early[Q2_PART[e]], metric_row(metric, e), rows) - early[Q2[i]]
        )
    sent = [
        (k * E, E, early[place[7]], early[place[0]])
        for k, place in enumerate((Q1, Q2_PART, V2_PART))
    ]
    sent.append((T, L, inverses[7], inverses[0]))
    sent.append((W + 3, 1, metric_row(metric, 7), metric_row(metric, 0)))
    for base, size, high, low in sent:
        pair[base : base + size] = jnp.where(even, high, low)
        cross[base : base + size] = jnp.where(end, 0.0, jnp.where(even, low, high))


def partial(a, b):
    return jnp.sum((a[:W] * b[:W]).reshape(W // 8, 8, L), 0)


def gram(depth, other):
    return 3 + depth * (depth + 1) // 2 + other


def tally(sums, depth, first, images, result):
    sums[depth] = sums[depth] + partial(first, result)
    for other in range(depth):
        k = gram(depth, other)
        sums[k] = sums[k] + partial(images[other], result)
    k = gram(depth, depth)
    sums[k] = sums[k] + partial(result, result)


def direction_of(search, new_search, early, depth, j):
    if depth == 0:
        return (early, Q1[j]) if j in Q1 else (search, 0, j)
    if 2 <= j <= 5:
        return (search, depth, j)
    return (early, Q2[j]) if depth == 1 and j in Q2 else (new_search, depth, j)


def image_of(field, new_field, early, depth, j):
    if depth == 0 and j in V1:
        return (early, V1[j])
    inner = 3 <= j <= 4 if depth == 2 else 2 <= j <= 5
    return (field if inner else new_field, depth, j)


def read(place, *more):
    return place[0][(*place[1:], *more)]


def inner_kernel(
    metric, vertical, inverses, cells, edges, early, search, field, totals, middle, advected, ring
):
    rows = vertical_rows(vertical)
    rim = cells[:, 2 * R].reshape(L, 128).T
    for j in range(R):
        if edge(j):
            ring[j] = edges[j]
        else:
            turned_row(cells, rim, j, ring, j)
            middle[j - H] = ring[j]
        advected[row_of(j), :] = ring[j, :W]
    sums = [jnp.zeros((8, L), jnp.float32) for _ in range(9)]

    def q(depth, j):
        return read(direction_of(search, None, early, depth, j))

    def v(depth, j):
        return read(image_of(field, None, early, depth, j))

    for depth, solved, applied in ((0, (3, 4), range(2, 6)), (1, range(2, 6), range(2, 6)), (2, range(2, 6), (3, 4))):
        for j in solved:
            search[depth, j] = precondition(
                inverses[j], ring[j] if depth == 0 else v(depth - 1, j)
            )
        for j in applied:
            field[depth, j] = operate(
                q(depth, j), q(depth, j - 1), q(depth, j + 1), metric_row(metric, j), rows
            )
        for j in (1, *applied, 6) if depth == 0 else applied:
            tally(sums, depth, ring[j], [v(o, j) for o in range(depth)], v(depth, j))
    for k in range(9):
        totals[k] = sums[k]


def outer_kernel(
    metric, vertical, inverses, edges, pair, cross, early, search, field, totals,
    new_search, new_field, sums_out,
):
    even = is_even()
    lane = lax.broadcasted_iota(jnp.int32, (1, L), 1)
    rows = vertical_rows(vertical)
    sums = [totals[k] for k in range(9)]

    def beyond(e, base, size):
        part = slice(base, base + size)
        first, second = (cross, pair) if e == 0 else (pair, cross)
        return jnp.where(even, first[part], second[part])

    def q(depth, j):
        return read(direction_of(search, new_search, early, depth, j))

    def v(depth, j):
        return read(image_of(field, new_field, early, depth, j))

    def add(depth, j):
        tally(sums, depth, edges[j], [v(o, j) for o in range(depth)], v(depth, j))

    def apply(depth, j, south_or_north, other):
        new_field[depth, j] = operate(
            q(depth, j), south_or_north, other, metric_row(metric, j), rows
        )
        add(depth, j)

    outside = []
    for e, _, _, _ in ENDS:
        outside.append(
            (
                beyond(e, T, L),
                beyond(e, W + 3, 1),
                precondition(beyond(e, T, L), early[Q1[e]]),
            )
        )
        new_field[0, e] = early[V1_PART[e]] - beyond(e, 0, E)
        add(0, e)
    for e, _, _, _ in ENDS:
        new_search[1, e] = precondition(inverses[e], new_field[0, e])
    last = []
    for (e, i, i2, _), (inverse, m, extra) in zip(ENDS, outside):
        apply(1, e, q(1, i), beyond(e, E, E) - extra)
        apply(1, i, q(1, e), q(1, i2))
        image = beyond(e, 2 * E, E) - alone(extra, m, rows) - q(1, e)
        last.append(precondition(inverse, image))
    for e, i, _, _ in ENDS:
        new_search[2, e] = precondition(inverses[e], new_field[1, e])
        new_search[2, i] = precondition(inverses[i], new_field[1, i])
    for (e, i, i2, i3), far in zip(ENDS, last):
        apply(2, e, q(2, i), far)
        apply(2, i, q(2, e), q(2, i2))
        apply(2, i2, q(2, i), q(2, i3))
    row = jnp.zeros((1, L), jnp.float32)
    for k in range(9):
        total = jnp.sum(jnp.sum(sums[k], 0, keepdims=True), 1, keepdims=True)
        row = jnp.where(lane == k, total, row)
    sums_out[...] = jnp.broadcast_to(row, sums_out.shape)


def finish_kernel(
    sums, edges, middle, early, search, field, new_search, new_field, pressure, residual,
    held, left, sems,
):
    lane = lax.broadcasted_iota(jnp.int32, (1, L), 1)
    row = jnp.sum(sums[...], 0, keepdims=True)

    def entry(index):
        value = jnp.sum(jnp.where(lane == index, row, 0.0), 1, keepdims=True)
        return jnp.broadcast_to(value, (1, L))

    b1, b2, b3, g11, g12, g22, g13, g23, g33 = (entry(i) for i in range(9))
    l21 = g12 / g11
    l31 = g13 / g11
    d2 = g22 - l21 * g12
    cross = g23 - l21 * g13
    l32 = cross / d2
    d3 = g33 - l31 * g13 - l32 * cross
    c2 = b2 - l21 * b1
    y1 = b1 / g11
    y2 = c2 / d2
    y3 = (b3 - l31 * b1 - l32 * c2) / d3
    k3 = y3
    k2 = y2 - l32 * k3
    k1 = y1 - l21 * k2 - l31 * k3
    parts = 4
    size = W // parts
    copies = []
    for part in range(parts):
        span = slice(part * size, (part + 1) * size)
        for j in range(R):
            q = [
                read(direction_of(search, new_search, early, depth, j), span)
                for depth in range(3)
            ]
            v = [
                read(image_of(field, new_field, early, depth, j), span)
                for depth in range(3)
            ]
            to = pl.ds(part * size * R + j, size, stride=R)
            held[to, :] = k1 * q[0] + k2 * q[1] + k3 * q[2]
            first = edges[j, span] if edge(j) else middle[j - H, span]
            left[to, :] = first - k1 * v[0] - k2 * v[1] - k3 * v[2]
        block = pl.ds(part * size * R, size * R)
        for i, (source, target) in enumerate(((held, pressure), (left, residual))):
            copy = pltpu.make_async_copy(
                source.at[block, :], target.at[block, :], sems.at[part, i]
            )
            copy.start()
            copies.append(copy)
    for copy in copies:
        copy.wait()


VMEM = pl.BlockSpec(memory_space=pltpu.VMEM)
SMEM = pl.BlockSpec(memory_space=pltpu.SMEM)
HBM = pl.BlockSpec(memory_space=pltpu.HBM)
ANY = pl.BlockSpec(memory_space=pl.ANY)


def call(
    kernel, ins, outs, scratch=(), limit=32, flops=0, where=VMEM, aliases=None, dtype=jnp.float32
):
    return pl.pallas_call(
        kernel,
        out_shape=tuple(jax.ShapeDtypeStruct(s, dtype) for s in outs),
        in_specs=list(ins),
        out_specs=tuple(where for _ in outs),
        scratch_shapes=[
            pltpu.VMEM(s, jnp.float32) if isinstance(s, tuple) else s for s in scratch
        ],
        input_output_aliases=aliases or {},
        compiler_params=pltpu.CompilerParams(vmem_limit_bytes=limit * MIB),
        cost_estimate=pl.CostEstimate(
            flops=flops, bytes_accessed=8 * MIB, transcendentals=0
        ),
    )


def body(count, tracer, offsets, frac_lon, frac_lat, frac_lev, metric, vertical_coef, inverses):
    in_chip = [(i, i ^ 1) for i in range(count)]
    across = [(i, (i - 1 + 2 * (i % 2)) % count) for i in range(count)]
    flat = tracer.reshape(W * R, L)
    pair_out, cross_out = call(edges_kernel, (VMEM,), ((2 * W, L), (2 * W, L)))(flat)
    cross_in = lax.ppermute(cross_out, LAT, across)
    pair_in = lax.ppermute(pair_out, LAT, in_chip)
    fractions = jnp.broadcast_to(
        jnp.concatenate([frac_lat, frac_lev])[:, None], (2 * R, L)
    )
    turned = None
    for kernel, n, extra in (
        (mix_core_kernel, 5, ()),
        (mix_side_kernel, 3, (pair_in, cross_in)),
    ):
        more = () if turned is None else (turned,)
        (turned,) = call(
            kernel,
            (VMEM,) * (2 + len(extra)) + (ANY,) * len(more),
            ((NL, 2, R, 8, 128),),
            scratch=((n, NL, 2, 8, 128), pltpu.SemaphoreType.DMA((n,))),
            where=ANY,
            aliases={4: 0} if more else None,
            flops=10**9,
        )(fractions, flat, *extra, *more)
    lines = lax.all_to_all(turned, LON, 0, 0, tiled=True)
    (moved,) = call(
        shift_kernel,
        (SMEM, SMEM, VMEM),
        ((NL, 2 * R + 1, 8, 128),),
        scratch=((R, 2 * B, 8, 128),),
    )(offsets, frac_lon, lines.reshape(B, R, 8, 128))
    back = lax.all_to_all(moved, LON, 0, 0, tiled=True)
    vertical = vertical_coef.reshape(1, L)
    edges, pair_out, cross_out, early = call(
        turn_kernel,
        (SMEM, VMEM, VMEM, VMEM),
        ((R, E, L), (T + L, L), (T + L, L), (EARLY, E, L)),
    )(metric, vertical, inverses, back)
    cross = lax.ppermute(cross_out, LAT, across)
    pair = lax.ppermute(pair_out, LAT, in_chip)
    search, images, totals, middle, advected = call(
        inner_kernel,
        (SMEM,) + (VMEM,) * 5,
        ((3, R, E, L), (3, R, E, L), (9, 8, L), (R - 2 * H, E, L), (W * R, L)),
        scratch=((R, E, L),),
        flops=2 * 10**9,
    )(metric, vertical, inverses, back, edges, early)
    new_search, new_images, sums = call(
        outer_kernel,
        (SMEM,) + (VMEM,) * 9,
        ((3, R, E, L), (3, R, E, L), (count * NL, L)),
    )(metric, vertical, inverses, edges, pair, cross, early, search, images, totals)
    gathered = lax.all_to_all(sums, LON_LAT, 0, 0, tiled=True)
    pressure, residual = call(
        finish_kernel,
        (VMEM,) * 8,
        ((W * R, L), (W * R, L)),
        scratch=((W * R, L), (W * R, L), pltpu.SemaphoreType.DMA((4, 2))),
        where=HBM,
    )(gathered, edges, middle, early, search, images, new_search, new_images)
    return tuple(x.reshape(W, R, L) for x in (advected, pressure, residual))


def solution(mesh):
    count = mesh.shape["lat"]
    split = Mesh(mesh.devices.reshape(4, 4, count // 2, 2), LON_LAT)
    placed = (P(LON, LAT, None), P(LAT), P(LAT), P(LAT), P(LAT), P(LAT), P(), P(LAT, None, None))
    return jax.shard_map(
        functools.partial(body, count),
        mesh=split,
        in_specs=placed,
        out_specs=(P(LON, LAT, None),) * 3,
        check_vma=False,
    )
```

```python
import functools

import jax
import jax.numpy as jnp
from jax import lax
from jax.experimental import pallas as pl
from jax.experimental.pallas import tpu as pltpu
from jax.sharding import Mesh
from jax.sharding import PartitionSpec as P

LON = ("lon_0", "lon_1")
LAT = ("lat_0", "lat_1")
LON_LAT = ("lon_0", "lon_1", "lat_0", "lat_1")
W = 256
R = 8
L = 128
H = 3
E = W + 8
NL = 16
B = 2 * NL
T = H * E
MIB = 1 << 20
CORE = (1, 2, 3, 4, 5)
SIDE = (0, 6, 7)


def weights(f):
    sixth = 1.0 / 6.0
    return (
        -f * (f - 1.0) * (f - 2.0) * sixth,
        (f + 1.0) * (f - 1.0) * (f - 2.0) * 0.5,
        -(f + 1.0) * f * (f - 2.0) * 0.5,
        (f + 1.0) * f * (f - 1.0) * sixth,
    )


def halves(x):
    high = x.astype(jnp.bfloat16)
    return high, (x - high.astype(jnp.float32)).astype(jnp.bfloat16)


def dot_nt(a, b):
    return lax.dot_general(
        a, b, (((1,), (1,)), ((), ())), preferred_element_type=jnp.float32
    )


def row_of(j):
    return pl.ds(j, W, stride=R)


def is_even():
    return lax.axis_index("lat_1") == 0


def at_end():
    place = 2 * lax.axis_index("lat_0") + lax.axis_index("lat_1")
    return (place == 0) | (place == 2 * lax.axis_size("lat_0") - 1)


def edges_kernel(tracer, pair, cross):
    even, end = is_even(), at_end()
    last = tracer[row_of(R - 1), :]
    first = tracer[row_of(0), :]
    second = tracer[row_of(1), :]
    pair[0:W] = jnp.where(even, last, first)
    pair[W : 2 * W] = second
    cross[0:W] = jnp.where(end, 0.0, jnp.where(even, first, last))
    cross[W : 2 * W] = jnp.where(end, 0.0, second)


def mix_rows(rows, row, fractions, held, out, sems):
    delta = lax.broadcasted_iota(jnp.int32, (L, L), 1) - lax.broadcasted_iota(
        jnp.int32, (L, L), 0
    )
    copies = []
    for at, j in enumerate(rows):
        w = weights(fractions[j : j + 1, :])
        mixed = w[0] * row(j - 1) + w[1] * row(j) + w[2] * row(j + 1) + w[3] * row(j + 2)
        v = weights(fractions[R + j : R + j + 1, :])
        table = jnp.zeros((L, L), jnp.float32)
        for m in range(4):
            table = jnp.where(delta == m - 1, v[m], table)
        t_high, t_low = halves(table)
        m_high, m_low = halves(mixed)
        left = jnp.concatenate(
            [
                jnp.concatenate([t_high, t_high], 1),
                jnp.concatenate([t_low, t_low], 1),
            ],
            0,
        )
        both = dot_nt(left, jnp.concatenate([m_high, m_low], 1))
        turned = (both[:L] + both[L:]).reshape(NL, 8, W)
        held[at, :, 0] = turned[:, :, :128]
        held[at, :, 1] = turned[:, :, 128:]
        copies.append(
            pltpu.make_async_copy(held.at[at], out.at[:, :, j], sems.at[at])
        )
        copies[-1].start()
    for copy in copies:
        copy.wait()


def mix_core_kernel(fractions, tracer, out, held, sems):
    mix_rows(CORE, lambda k: tracer[row_of(k), :], fractions, held, out, sems)


def mix_side_kernel(fractions, tracer, cross, pair, begun, out, held, sems):
    even = is_even()

    def row(k):
        if k < 0:
            return jnp.where(even, cross[0:W], pair[0:W])
        if k >= R:
            part = slice((k - R) * W, (k - R + 1) * W)
            return jnp.where(even, pair[part], cross[part])
        return tracer[row_of(k), :]

    mix_rows(SIDE, row, fractions, held, out, sems)


def shift_kernel(offsets, frac_lon, cells, out, twice):
    delta = lax.broadcasted_iota(jnp.int32, (128, 128), 0) - lax.broadcasted_iota(
        jnp.int32, (128, 128), 1
    )
    lane = lax.broadcasted_iota(jnp.int32, (1, 1, 128), 2)
    rims = jnp.zeros((NL, 8, 128), jnp.float32)
    for j in range(R):
        w = weights(frac_lon[j])
        off = offsets[j]
        turns = lax.shift_right_logical(off, 7)
        rest = jnp.bitwise_and(off, 127)
        placed = delta + rest
        left, right_high, right_low = [], [], []
        for k in range(3):
            table = jnp.zeros((128, 128), jnp.float32)
            for m in range(4):
                table = jnp.where(placed == m - 1 - 128 * (k - 1), w[m], table)
            t_high, t_low = halves(table)
            right_high += [t_high, t_high]
            right_low += [t_low, t_low]
            if k == 0:
                part = jnp.concatenate([cells[B - 1 :, j], cells[: B - 1, j]], 0)
            elif k == 1:
                part = cells[:, j]
            else:
                part = jnp.concatenate([cells[1:, j], cells[:1, j]], 0)
            left += list(halves(part.reshape(B * 8, 128)))
        right = jnp.concatenate(
            [jnp.concatenate(right_high, 0), jnp.concatenate(right_low, 0)], 1
        )
        both = jnp.dot(
            jnp.concatenate(left, 1), right, preferred_element_type=jnp.float32
        )
        value = (both[:, :128] + both[:, 128:]).reshape(B, 8, 128)
        twice[j, :B] = value
        twice[j, B:] = value
        start = jnp.bitwise_and(B - turns, B - 1)
        moved = twice[j, pl.ds(start, B)].reshape(NL, 2, 8, 128)
        near, far = moved[:, 0], moved[:, 1]
        out[:, j] = near
        out[:, R + j] = far
        east = jnp.concatenate([near[1:], near[:1]], 0)
        west = jnp.concatenate([far[NL - 1 :], far[: NL - 1]], 0)
        rim = jnp.where(lane < 64, east, west)
        if j > 0:
            rim = pltpu.roll(rim, 8 * j, 2)
        rims = jnp.where(jnp.bitwise_and(lane + (4 - 8 * j), 127) < 8, rim, rims)
    out[:, 2 * R] = rims


def edge(j):
    return j < H or j >= R - H


def turned_row(cells, rim, j, ref, at):
    sub = lax.broadcasted_iota(jnp.int32, (8, L), 0)
    for h in range(2):
        ref[at, h * 128 : (h + 1) * 128, :] = cells[:, h * R + j].reshape(L, 128).T
    before = (8 * j - 8) % 128
    tail = jnp.where(sub < 4, rim[8 * j : 8 * j + 8], rim[before : before + 8])
    ref[at, W:E, :] = tail


def vertical_rows(vertical):
    lane = lax.broadcasted_iota(jnp.int32, (1, L), 1)
    coef = vertical[...]
    return coef, jnp.where(lane == L - 1, 0.0, coef), jnp.where(lane == 0, 0.0, coef)


def precondition(inverse, value):
    m_high, m_low = halves(inverse)
    v_high, v_low = halves(value)
    right = jnp.concatenate(
        [
            jnp.concatenate([m_high, m_high], 1),
            jnp.concatenate([m_low, m_low], 1),
        ],
        0,
    )
    both = dot_nt(jnp.concatenate([v_high, v_low], 1), right)
    return both[:, :L] + both[:, L:]


def alone(q, m, rows):
    coef, upper, lower = rows
    result = q * (2.0 * m + 2.0 * coef + 2.1)
    result = result - m * (pltpu.roll(q, 1, 0) + pltpu.roll(q, E - 1, 0))
    result = result - upper * pltpu.roll(q, L - 1, 1)
    return result - lower * pltpu.roll(q, 1, 1)


def operate(q, south, north, m, rows):
    return alone(q, m, rows) - (south + north)


def metric_row(metric, j):
    return jnp.full((1, L), metric[j], jnp.float32)


Q1 = {0: 0, 1: 1, 2: 2, 5: 3, 6: 4, 7: 5}
V1_PART = {0: 6, 7: 7}
V1 = {1: 8, 6: 9}
Q2_PART = {0: 10, 7: 11}
Q2 = {1: 12, 6: 13}
V2_PART = {0: 14, 7: 15}
EARLY = 16
ENDS = ((0, 1, 2, 3), (7, 6, 5, 4))


def turn_kernel(metric, vertical, inverses, cells, ring, cross, early):
    even, end = is_even(), at_end()
    rows = vertical_rows(vertical)
    rim = cells[:, 2 * R].reshape(L, 128).T
    for j in range(R):
        if edge(j):
            turned_row(cells, rim, j, ring, j)
            early[Q1[j]] = precondition(inverses[j], ring[j])
    for e, i, i2, _ in ENDS:
        early[V1_PART[e]] = alone(early[Q1[e]], metric_row(metric, e), rows) - early[Q1[i]]
        early[V1[i]] = operate(
            early[Q1[i]], early[Q1[e]], early[Q1[i2]], metric_row(metric, i), rows
        )
    for e, i, _, _ in ENDS:
        early[Q2_PART[e]] = precondition(inverses[e], early[V1_PART[e]])
        early[Q2[i]] = precondition(inverses[i], early[V1[i]])
    for e, i, _, _ in ENDS:
        early[V2_PART[e]] = (
            alone(early[Q2_PART[e]], metric_row(metric, e), rows) - early[Q2[i]]
        )
    for base, size, high, low in sent_rows(metric, inverses, early):
        cross[base : base + size] = jnp.where(end, 0.0, jnp.where(even, low, high))


def sent_rows(metric, inverses, early):
    sent = [
        (k * E, E, early[place[7]], early[place[0]])
        for k, place in enumerate((Q1, Q2_PART, V2_PART))
    ]
    sent.append((T, L, inverses[7], inverses[0]))
    sent.append((W + 3, 1, metric_row(metric, 7), metric_row(metric, 0)))
    return sent


def partial(a, b):
    return jnp.sum((a[:W] * b[:W]).reshape(W // 8, 8, L), 0)


def gram(depth, other):
    return 3 + depth * (depth + 1) // 2 + other


def tally(sums, depth, first, images, result):
    sums[depth] = sums[depth] + partial(first, result)
    for other in range(depth):
        k = gram(depth, other)
        sums[k] = sums[k] + partial(images[other], result)
    k = gram(depth, depth)
    sums[k] = sums[k] + partial(result, result)


def direction_of(search, new_search, early, depth, j):
    if depth == 0:
        return (early, Q1[j]) if j in Q1 else (search, 0, j)
    if 2 <= j <= 5:
        return (search, depth, j)
    return (early, Q2[j]) if depth == 1 and j in Q2 else (new_search, depth, j)


def image_of(field, new_field, early, depth, j):
    if depth == 0 and j in V1:
        return (early, V1[j])
    inner = 3 <= j <= 4 if depth == 2 else 2 <= j <= 5
    return (field if inner else new_field, depth, j)


def read(place, *more):
    return place[0][(*place[1:], *more)]


def inner_kernel(
    metric, vertical, inverses, cells, edges, early,
    search, field, totals, middle, advected, pair, ring,
):
    for base, size, high, low in sent_rows(metric, inverses, early):
        pair[base : base + size] = jnp.where(is_even(), high, low)
    rows = vertical_rows(vertical)
    rim = cells[:, 2 * R].reshape(L, 128).T
    for j in range(R):
        if edge(j):
            ring[j] = edges[j]
        else:
            turned_row(cells, rim, j, ring, j)
            middle[j - H] = ring[j]
        advected[row_of(j), :] = ring[j, :W]
    sums = [jnp.zeros((8, L), jnp.float32) for _ in range(9)]

    def q(depth, j):
        return read(direction_of(search, None, early, depth, j))

    def v(depth, j):
        return read(image_of(field, None, early, depth, j))

    for depth, solved, applied in ((0, (3, 4), range(2, 6)), (1, range(2, 6), range(2, 6)), (2, range(2, 6), (3, 4))):
        for j in solved:
            search[depth, j] = precondition(
                inverses[j], ring[j] if depth == 0 else v(depth - 1, j)
            )
        for j in applied:
            field[depth, j] = operate(
                q(depth, j), q(depth, j - 1), q(depth, j + 1), metric_row(metric, j), rows
            )
        for j in (1, *applied, 6) if depth == 0 else applied:
            tally(sums, depth, ring[j], [v(o, j) for o in range(depth)], v(depth, j))
    for k in range(9):
        totals[k] = sums[k]


def outer_kernel(
    metric, vertical, inverses, edges, pair, cross, early, search, field, totals,
    new_search, new_field, sums_out,
):
    even = is_even()
    lane = lax.broadcasted_iota(jnp.int32, (1, L), 1)
    rows = vertical_rows(vertical)
    sums = [totals[k] for k in range(9)]

    def beyond(e, base, size):
        part = slice(base, base + size)
        first, second = (cross, pair) if e == 0 else (pair, cross)
        return jnp.where(even, first[part], second[part])

    def q(depth, j):
        return read(direction_of(search, new_search, early, depth, j))

    def v(depth, j):
        return read(image_of(field, new_field, early, depth, j))

    def add(depth, j):
        tally(sums, depth, edges[j], [v(o, j) for o in range(depth)], v(depth, j))

    def apply(depth, j, south_or_north, other):
        new_field[depth, j] = operate(
            q(depth, j), south_or_north, other, metric_row(metric, j), rows
        )
        add(depth, j)

    outside = []
    for e, _, _, _ in ENDS:
        outside.append(
            (
                beyond(e, T, L),
                beyond(e, W + 3, 1),
                precondition(beyond(e, T, L), early[Q1[e]]),
            )
        )
        new_field[0, e] = early[V1_PART[e]] - beyond(e, 0, E)
        add(0, e)
    for e, _, _, _ in ENDS:
        new_search[1, e] = precondition(inverses[e], new_field[0, e])
    last = []
    for (e, i, i2, _), (inverse, m, extra) in zip(ENDS, outside):
        apply(1, e, q(1, i), beyond(e, E, E) - extra)
        apply(1, i, q(1, e), q(1, i2))
        image = beyond(e, 2 * E, E) - alone(extra, m, rows) - q(1, e)
        last.append(precondition(inverse, image))
    for e, i, _, _ in ENDS:
        new_search[2, e] = precondition(inverses[e], new_field[1, e])
        new_search[2, i] = precondition(inverses[i], new_field[1, i])
    for (e, i, i2, i3), far in zip(ENDS, last):
        apply(2, e, q(2, i), far)
        apply(2, i, q(2, e), q(2, i2))
        apply(2, i2, q(2, i), q(2, i3))
    row = jnp.zeros((1, L), jnp.float32)
    for k in range(9):
        total = jnp.sum(jnp.sum(sums[k], 0, keepdims=True), 1, keepdims=True)
        row = jnp.where(lane == k, total, row)
    sums_out[...] = jnp.broadcast_to(row, sums_out.shape)


def finish_kernel(
    sums, edges, middle, early, search, field, new_search, new_field, pressure, residual,
    held, left, sems,
):
    lane = lax.broadcasted_iota(jnp.int32, (1, L), 1)
    row = jnp.sum(sums[...], 0, keepdims=True)

    def entry(index):
        value = jnp.sum(jnp.where(lane == index, row, 0.0), 1, keepdims=True)
        return jnp.broadcast_to(value, (1, L))

    b1, b2, b3, g11, g12, g22, g13, g23, g33 = (entry(i) for i in range(9))
    l21 = g12 / g11
    l31 = g13 / g11
    d2 = g22 - l21 * g12
    cross = g23 - l21 * g13
    l32 = cross / d2
    d3 = g33 - l31 * g13 - l32 * cross
    c2 = b2 - l21 * b1
    y1 = b1 / g11
    y2 = c2 / d2
    y3 = (b3 - l31 * b1 - l32 * c2) / d3
    k3 = y3
    k2 = y2 - l32 * k3
    k1 = y1 - l21 * k2 - l31 * k3
    parts = 4
    size = W // parts
    copies = []
    for part in range(parts):
        span = slice(part * size, (part + 1) * size)
        for j in range(R):
            q = [
                read(direction_of(search, new_search, early, depth, j), span)
                for depth in range(3)
            ]
            v = [
                read(image_of(field, new_field, early, depth, j), span)
                for depth in range(3)
            ]
            to = pl.ds(part * size * R + j, size, stride=R)
            held[to, :] = k1 * q[0] + k2 * q[1] + k3 * q[2]
            first = edges[j, span] if edge(j) else middle[j - H, span]
            left[to, :] = first - k1 * v[0] - k2 * v[1] - k3 * v[2]
        block = pl.ds(part * size * R, size * R)
        for i, (source, target) in enumerate(((held, pressure), (left, residual))):
            copy = pltpu.make_async_copy(
                source.at[block, :], target.at[block, :], sems.at[part, i]
            )
            copy.start()
            copies.append(copy)
    for copy in copies:
        copy.wait()


VMEM = pl.BlockSpec(memory_space=pltpu.VMEM)
SMEM = pl.BlockSpec(memory_space=pltpu.SMEM)
HBM = pl.BlockSpec(memory_space=pltpu.HBM)
ANY = pl.BlockSpec(memory_space=pl.ANY)


def call(
    kernel, ins, outs, scratch=(), limit=32, flops=0, where=(), aliases=None, dtype=jnp.float32
):
    return pl.pallas_call(
        kernel,
        out_shape=tuple(jax.ShapeDtypeStruct(s, dtype) for s in outs),
        in_specs=list(ins),
        out_specs=where or (VMEM,) * len(outs),
        scratch_shapes=[
            pltpu.VMEM(s, jnp.float32) if isinstance(s, tuple) else s for s in scratch
        ],
        input_output_aliases=aliases or {},
        compiler_params=pltpu.CompilerParams(vmem_limit_bytes=limit * MIB),
        cost_estimate=pl.CostEstimate(
            flops=flops, bytes_accessed=8 * MIB, transcendentals=0
        ),
    )


def body(count, tracer, offsets, frac_lon, frac_lat, frac_lev, metric, vertical_coef, inverses):
    in_chip = [(i, i ^ 1) for i in range(count)]
    across = [(i, (i - 1 + 2 * (i % 2)) % count) for i in range(count)]
    flat = tracer.reshape(W * R, L)
    pair_out, cross_out = call(edges_kernel, (VMEM,), ((2 * W, L), (2 * W, L)))(flat)
    pair_in = lax.ppermute(pair_out, LAT, in_chip)
    cross_in = lax.ppermute(cross_out, LAT, across)
    fractions = jnp.broadcast_to(
        jnp.concatenate([frac_lat, frac_lev])[:, None], (2 * R, L)
    )
    (begun,) = call(
        mix_core_kernel,
        (VMEM,) * 2,
        ((NL, 2, R, 8, 128),),
        scratch=((5, NL, 2, 8, 128), pltpu.SemaphoreType.DMA((5,))),
        where=(ANY,),
        flops=10**9,
    )(fractions, flat)
    (turned,) = call(
        mix_side_kernel,
        (VMEM,) * 4 + (ANY,),
        ((NL, 2, R, 8, 128),),
        scratch=((3, NL, 2, 8, 128), pltpu.SemaphoreType.DMA((3,))),
        where=(ANY,),
        aliases={4: 0},
    )(fractions, flat, cross_in, pair_in, begun)
    lines = lax.all_to_all(turned, LON, 0, 0, tiled=True)
    (moved,) = call(
        shift_kernel,
        (SMEM, SMEM, VMEM),
        ((NL, 2 * R + 1, 8, 128),),
        scratch=((R, 2 * B, 8, 128),),
    )(offsets, frac_lon, lines.reshape(B, R, 8, 128))
    back = lax.all_to_all(moved, LON, 0, 0, tiled=True)
    vertical = vertical_coef.reshape(1, L)
    edges, cross_out, early = call(
        turn_kernel,
        (SMEM, VMEM, VMEM, VMEM),
        ((R, E, L), (T + L, L), (EARLY, E, L)),
    )(metric, vertical, inverses, back)
    cross = lax.ppermute(cross_out, LAT, across)
    search, images, totals, middle, advected, pair_out = call(
        inner_kernel,
        (SMEM,) + (VMEM,) * 5,
        ((3, R, E, L), (3, R, E, L), (9, 8, L), (R - 2 * H, E, L), (W * R, L), (T + L, L)),
        scratch=((R, E, L),),
        flops=2 * 10**9,
    )(metric, vertical, inverses, back, edges, early)
    pair = lax.ppermute(pair_out, LAT, in_chip)
    new_search, new_images, sums = call(
        outer_kernel,
        (SMEM,) + (VMEM,) * 9,
        ((3, R, E, L), (3, R, E, L), (count * NL, L)),
    )(metric, vertical, inverses, edges, pair, cross, early, search, images, totals)
    gathered = lax.all_to_all(sums, LON_LAT, 0, 0, tiled=True)
    pressure, residual = call(
        finish_kernel,
        (VMEM,) * 8,
        ((W * R, L), (W * R, L)),
        scratch=((W * R, L), (W * R, L), pltpu.SemaphoreType.DMA((4, 2))),
        where=(HBM, HBM),
    )(gathered, edges, middle, early, search, images, new_search, new_images)
    return tuple(x.reshape(W, R, L) for x in (advected, pressure, residual))


def solution(mesh):
    count = mesh.shape["lat"]
    split = Mesh(mesh.devices.reshape(4, 4, count // 2, 2), LON_LAT)
    placed = (P(LON, LAT, None), P(LAT), P(LAT), P(LAT), P(LAT), P(LAT), P(), P(LAT, None, None))
    return jax.shard_map(
        functools.partial(body, count),
        mesh=split,
        in_specs=placed,
        out_specs=(P(LON, LAT, None),) * 3,
        check_vma=False,
    )
```

```python
import functools

import jax
import jax.numpy as jnp
from jax import lax
from jax.experimental import pallas as pl
from jax.experimental.pallas import tpu as pltpu
from jax.sharding import Mesh
from jax.sharding import PartitionSpec as P

LON = ("lon_0", "lon_1")
LAT = ("lat_0", "lat_1")
LON_LAT = ("lon_0", "lon_1", "lat_0", "lat_1")
W = 256
R = 8
L = 128
H = 3
E = W + 8
NL = 16
B = 2 * NL
T = H * E
MIB = 1 << 20
CORE = (1, 2, 3, 4, 5)
SIDE = (0, 6, 7)


def weights(f):
    sixth = 1.0 / 6.0
    return (
        -f * (f - 1.0) * (f - 2.0) * sixth,
        (f + 1.0) * (f - 1.0) * (f - 2.0) * 0.5,
        -(f + 1.0) * f * (f - 2.0) * 0.5,
        (f + 1.0) * f * (f - 1.0) * sixth,
    )


def halves(x):
    high = x.astype(jnp.bfloat16)
    return high, (x - high.astype(jnp.float32)).astype(jnp.bfloat16)


def dot_nt(a, b):
    return lax.dot_general(
        a, b, (((1,), (1,)), ((), ())), preferred_element_type=jnp.float32
    )


def row_of(j):
    return pl.ds(j, W, stride=R)


def is_even():
    return lax.axis_index("lat_1") == 0


def at_end():
    place = 2 * lax.axis_index("lat_0") + lax.axis_index("lat_1")
    return (place == 0) | (place == 2 * lax.axis_size("lat_0") - 1)


def edges_kernel(tracer, pair, cross):
    even, end = is_even(), at_end()
    last = tracer[row_of(R - 1), :]
    first = tracer[row_of(0), :]
    second = tracer[row_of(1), :]
    pair[0:W] = jnp.where(even, last, first)
    pair[W : 2 * W] = second
    cross[0:W] = jnp.where(end, 0.0, jnp.where(even, first, last))
    cross[W : 2 * W] = jnp.where(end, 0.0, second)


def mix_rows(rows, row, fractions, held, out, sems):
    delta = lax.broadcasted_iota(jnp.int32, (L, L), 1) - lax.broadcasted_iota(
        jnp.int32, (L, L), 0
    )
    copies = []
    for at, j in enumerate(rows):
        w = weights(fractions[j : j + 1, :])
        mixed = w[0] * row(j - 1) + w[1] * row(j) + w[2] * row(j + 1) + w[3] * row(j + 2)
        v = weights(fractions[R + j : R + j + 1, :])
        table = jnp.zeros((L, L), jnp.float32)
        for m in range(4):
            table = jnp.where(delta == m - 1, v[m], table)
        t_high, t_low = halves(table)
        m_high, m_low = halves(mixed)
        left = jnp.concatenate(
            [
                jnp.concatenate([t_high, t_high], 1),
                jnp.concatenate([t_low, t_low], 1),
            ],
            0,
        )
        both = dot_nt(left, jnp.concatenate([m_high, m_low], 1))
        turned = (both[:L] + both[L:]).reshape(NL, 8, W)
        held[at, :, 0] = turned[:, :, :128]
        held[at, :, 1] = turned[:, :, 128:]
        copies.append(
            pltpu.make_async_copy(held.at[at], out.at[:, :, j], sems.at[at])
        )
        copies[-1].start()
    for copy in copies:
        copy.wait()


def mix_core_kernel(fractions, tracer, out, held, sems):
    mix_rows(CORE, lambda k: tracer[row_of(k), :], fractions, held, out, sems)


def mix_side_kernel(fractions, tracer, cross, pair, begun, out, held, sems):
    even = is_even()

    def row(k):
        if k < 0:
            return jnp.where(even, cross[0:W], pair[0:W])
        if k >= R:
            part = slice((k - R) * W, (k - R + 1) * W)
            return jnp.where(even, pair[part], cross[part])
        return tracer[row_of(k), :]

    mix_rows(SIDE, row, fractions, held, out, sems)


def shift_kernel(offsets, frac_lon, cells, out, twice):
    delta = lax.broadcasted_iota(jnp.int32, (128, 128), 0) - lax.broadcasted_iota(
        jnp.int32, (128, 128), 1
    )
    lane = lax.broadcasted_iota(jnp.int32, (1, 1, 128), 2)
    rims = jnp.zeros((NL, 8, 128), jnp.float32)
    for j in range(R):
        w = weights(frac_lon[j])
        off = offsets[j]
        turns = lax.shift_right_logical(off, 7)
        rest = jnp.bitwise_and(off, 127)
        placed = delta + rest
        left, right_high, right_low = [], [], []
        for k in range(3):
            table = jnp.zeros((128, 128), jnp.float32)
            for m in range(4):
                table = jnp.where(placed == m - 1 - 128 * (k - 1), w[m], table)
            t_high, t_low = halves(table)
            right_high += [t_high, t_high]
            right_low += [t_low, t_low]
            if k == 0:
                part = jnp.concatenate([cells[B - 1 :, j], cells[: B - 1, j]], 0)
            elif k == 1:
                part = cells[:, j]
            else:
                part = jnp.concatenate([cells[1:, j], cells[:1, j]], 0)
            left += list(halves(part.reshape(B * 8, 128)))
        right = jnp.concatenate(
            [jnp.concatenate(right_high, 0), jnp.concatenate(right_low, 0)], 1
        )
        both = jnp.dot(
            jnp.concatenate(left, 1), right, preferred_element_type=jnp.float32
        )
        value = (both[:, :128] + both[:, 128:]).reshape(B, 8, 128)
        twice[j, :B] = value
        twice[j, B:] = value
        start = jnp.bitwise_and(B - turns, B - 1)
        moved = twice[j, pl.ds(start, B)].reshape(NL, 2, 8, 128)
        near, far = moved[:, 0], moved[:, 1]
        out[:, j] = near
        out[:, R + j] = far
        east = jnp.concatenate([near[1:], near[:1]], 0)
        west = jnp.concatenate([far[NL - 1 :], far[: NL - 1]], 0)
        rim = jnp.where(lane < 64, east, west)
        if j > 0:
            rim = pltpu.roll(rim, 8 * j, 2)
        rims = jnp.where(jnp.bitwise_and(lane + (4 - 8 * j), 127) < 8, rim, rims)
    out[:, 2 * R] = rims


def turned_row(cells, rim, j, ref, at):
    sub = lax.broadcasted_iota(jnp.int32, (8, L), 0)
    for h in range(2):
        ref[at, h * 128 : (h + 1) * 128, :] = cells[:, h * R + j].reshape(L, 128).T
    here = pl.multiple_of(8 * j, 8)
    before = pl.multiple_of(jnp.bitwise_and(8 * j + 120, 127), 8)
    ref[at, W:E, :] = jnp.where(sub < 4, rim[pl.ds(here, 8), :], rim[pl.ds(before, 8), :])


def vertical_rows(vertical):
    lane = lax.broadcasted_iota(jnp.int32, (1, L), 1)
    coef = vertical[...]
    return coef, jnp.where(lane == L - 1, 0.0, coef), jnp.where(lane == 0, 0.0, coef)


def precondition(inverse, value):
    m_high, m_low = halves(inverse)
    v_high, v_low = halves(value)
    right = jnp.concatenate(
        [
            jnp.concatenate([m_high, m_high], 1),
            jnp.concatenate([m_low, m_low], 1),
        ],
        0,
    )
    both = dot_nt(jnp.concatenate([v_high, v_low], 1), right)
    return both[:, :L] + both[:, L:]


def alone(q, m, rows):
    coef, upper, lower = rows
    result = q * (2.0 * m + 2.0 * coef + 2.1)
    result = result - m * (pltpu.roll(q, 1, 0) + pltpu.roll(q, E - 1, 0))
    result = result - upper * pltpu.roll(q, L - 1, 1)
    return result - lower * pltpu.roll(q, 1, 1)


def operate(q, south, north, m, rows):
    return alone(q, m, rows) - (south + north)


def metric_row(metric, j):
    return jnp.full((1, L), metric[j], jnp.float32)


Q1 = {0: 0, 1: 1, 2: 2, 7: 8, 6: 9, 5: 10}
V1_PART = {0: 3, 7: 11}
V1 = {1: 4, 6: 12}
Q2_PART = {0: 5, 7: 13}
Q2 = {1: 6, 6: 14}
V2_PART = {0: 7, 7: 15}
EARLY = 8
ENDS = ((0, 1, 2, 3), (7, 6, 5, 4))


def row_at(end, k):
    return jnp.where(end == 0, k, R - 1 - k)


def solve_end(end, metric, rows, inverses, cells, rim, ring, at, early, base):
    j = [row_at(end, k) for k in range(H)]
    for k in range(H):
        turned_row(cells, rim, j[k], ring, at(k))
        early[base + k] = precondition(inverses[j[k]], ring[at(k)])
    m0, m1 = metric_row(metric, j[0]), metric_row(metric, j[1])
    early[base + 3] = alone(early[base], m0, rows) - early[base + 1]
    early[base + 4] = operate(early[base + 1], early[base], early[base + 2], m1, rows)
    early[base + 5] = precondition(inverses[j[0]], early[base + 3])
    early[base + 6] = precondition(inverses[j[1]], early[base + 4])
    early[base + 7] = alone(early[base + 5], m0, rows) - early[base + 6]


def fill(out, end, metric, inverses, early, base, blank=None):
    j = row_at(end, 0)
    sent = [(n * E, E, early[base + k]) for n, k in enumerate((0, 5, 7))]
    sent += [(T, L, inverses[j]), (W + 3, 1, metric_row(metric, j))]
    for start, size, value in sent:
        value = value if blank is None else jnp.where(blank, 0.0, value)
        out[start : start + size] = value


def turn_kernel(metric, vertical, inverses, cells, ring, cross, early, rim):
    rim[...] = cells[:, 2 * R].reshape(L, 128).T
    end = jnp.where(is_even(), 0, 1)
    solve_end(
        end, metric, vertical_rows(vertical), inverses, cells, rim, ring, lambda k: k, early, 0
    )
    fill(cross, end, metric, inverses, early, 0, at_end())


def partial(a, b):
    return jnp.sum((a[:W] * b[:W]).reshape(W // 8, 8, L), 0)


def gram(depth, other):
    return 3 + depth * (depth + 1) // 2 + other


def tally(sums, depth, first, images, result):
    sums[depth] = sums[depth] + partial(first, result)
    for other in range(depth):
        k = gram(depth, other)
        sums[k] = sums[k] + partial(images[other], result)
    k = gram(depth, depth)
    sums[k] = sums[k] + partial(result, result)


def direction_of(search, new_search, early, depth, j):
    if depth == 0:
        return (early, Q1[j]) if j in Q1 else (search, 0, j)
    if 2 <= j <= 5:
        return (search, depth, j)
    return (early, Q2[j]) if depth == 1 and j in Q2 else (new_search, depth, j)


def image_of(field, new_field, early, depth, j):
    if depth == 0 and j in V1:
        return (early, V1[j])
    inner = 3 <= j <= 4 if depth == 2 else 2 <= j <= 5
    return (field if inner else new_field, depth, j)


def read(place, *more):
    return place[0][(*place[1:], *more)]


def inner_kernel(
    metric, vertical, inverses, cells, turned, begun,
    search, field, totals, ring, early, advected, pair, rim,
):
    rows = vertical_rows(vertical)
    rim[...] = cells[:, 2 * R].reshape(L, 128).T
    across = jnp.where(is_even(), 0, 1)
    for k in range(H):
        ring[row_at(across, k)] = turned[k]
    for k in range(EARLY):
        early[EARLY * across + k] = begun[k]
    end = 1 - across
    solve_end(
        end, metric, rows, inverses, cells, rim, ring,
        lambda k: row_at(end, k), early, EARLY * end,
    )
    fill(pair, end, metric, inverses, early, EARLY * end)
    for j in range(H, R - H):
        turned_row(cells, rim, j, ring, j)
    for j in range(R):
        advected[row_of(j), :] = ring[j, :W]
    sums = [jnp.zeros((8, L), jnp.float32) for _ in range(9)]

    def q(depth, j):
        return read(direction_of(search, None, early, depth, j))

    def v(depth, j):
        return read(image_of(field, None, early, depth, j))

    for depth, solved, applied in ((0, (3, 4), range(2, 6)), (1, range(2, 6), range(2, 6)), (2, range(2, 6), (3, 4))):
        for j in solved:
            search[depth, j] = precondition(
                inverses[j], ring[j] if depth == 0 else v(depth - 1, j)
            )
        for j in applied:
            field[depth, j] = operate(
                q(depth, j), q(depth, j - 1), q(depth, j + 1), metric_row(metric, j), rows
            )
        for j in (1, *applied, 6) if depth == 0 else applied:
            tally(sums, depth, ring[j], [v(o, j) for o in range(depth)], v(depth, j))
    for k in range(9):
        totals[k] = sums[k]


def outer_kernel(
    metric, vertical, inverses, edges, pair, cross, early, search, field, totals,
    new_search, new_field, sums_out,
):
    even = is_even()
    lane = lax.broadcasted_iota(jnp.int32, (1, L), 1)
    rows = vertical_rows(vertical)
    sums = [totals[k] for k in range(9)]

    def beyond(e, base, size):
        part = slice(base, base + size)
        first, second = (cross, pair) if e == 0 else (pair, cross)
        return jnp.where(even, first[part], second[part])

    def q(depth, j):
        return read(direction_of(search, new_search, early, depth, j))

    def v(depth, j):
        return read(image_of(field, new_field, early, depth, j))

    def add(depth, j):
        tally(sums, depth, edges[j], [v(o, j) for o in range(depth)], v(depth, j))

    def apply(depth, j, south_or_north, other):
        new_field[depth, j] = operate(
            q(depth, j), south_or_north, other, metric_row(metric, j), rows
        )
        add(depth, j)

    outside = []
    for e, _, _, _ in ENDS:
        outside.append(
            (
                beyond(e, T, L),
                beyond(e, W + 3, 1),
                precondition(beyond(e, T, L), early[Q1[e]]),
            )
        )
        new_field[0, e] = early[V1_PART[e]] - beyond(e, 0, E)
        add(0, e)
    for e, _, _, _ in ENDS:
        new_search[1, e] = precondition(inverses[e], new_field[0, e])
    last = []
    for (e, i, i2, _), (inverse, m, extra) in zip(ENDS, outside):
        apply(1, e, q(1, i), beyond(e, E, E) - extra)
        apply(1, i, q(1, e), q(1, i2))
        image = beyond(e, 2 * E, E) - alone(extra, m, rows) - q(1, e)
        last.append(precondition(inverse, image))
    for e, i, _, _ in ENDS:
        new_search[2, e] = precondition(inverses[e], new_field[1, e])
        new_search[2, i] = precondition(inverses[i], new_field[1, i])
    for (e, i, i2, i3), far in zip(ENDS, last):
        apply(2, e, q(2, i), far)
        apply(2, i, q(2, e), q(2, i2))
        apply(2, i2, q(2, i), q(2, i3))
    row = jnp.zeros((1, L), jnp.float32)
    for k in range(9):
        total = jnp.sum(jnp.sum(sums[k], 0, keepdims=True), 1, keepdims=True)
        row = jnp.where(lane == k, total, row)
    sums_out[...] = jnp.broadcast_to(row, sums_out.shape)


def finish_kernel(
    sums, edges, early, search, field, new_search, new_field, pressure, residual,
    held, left, sems,
):
    lane = lax.broadcasted_iota(jnp.int32, (1, L), 1)
    row = jnp.sum(sums[...], 0, keepdims=True)

    def entry(index):
        value = jnp.sum(jnp.where(lane == index, row, 0.0), 1, keepdims=True)
        return jnp.broadcast_to(value, (1, L))

    b1, b2, b3, g11, g12, g22, g13, g23, g33 = (entry(i) for i in range(9))
    l21 = g12 / g11
    l31 = g13 / g11
    d2 = g22 - l21 * g12
    cross = g23 - l21 * g13
    l32 = cross / d2
    d3 = g33 - l31 * g13 - l32 * cross
    c2 = b2 - l21 * b1
    y1 = b1 / g11
    y2 = c2 / d2
    y3 = (b3 - l31 * b1 - l32 * c2) / d3
    k3 = y3
    k2 = y2 - l32 * k3
    k1 = y1 - l21 * k2 - l31 * k3
    parts = 4
    size = W // parts
    copies = []
    for part in range(parts):
        span = slice(part * size, (part + 1) * size)
        for j in range(R):
            q = [
                read(direction_of(search, new_search, early, depth, j), span)
                for depth in range(3)
            ]
            v = [
                read(image_of(field, new_field, early, depth, j), span)
                for depth in range(3)
            ]
            to = pl.ds(part * size * R + j, size, stride=R)
            held[to, :] = k1 * q[0] + k2 * q[1] + k3 * q[2]
            first = edges[j, span]
            left[to, :] = first - k1 * v[0] - k2 * v[1] - k3 * v[2]
        block = pl.ds(part * size * R, size * R)
        for i, (source, target) in enumerate(((held, pressure), (left, residual))):
            copy = pltpu.make_async_copy(
                source.at[block, :], target.at[block, :], sems.at[part, i]
            )
            copy.start()
            copies.append(copy)
    for copy in copies:
        copy.wait()


VMEM = pl.BlockSpec(memory_space=pltpu.VMEM)
SMEM = pl.BlockSpec(memory_space=pltpu.SMEM)
HBM = pl.BlockSpec(memory_space=pltpu.HBM)
ANY = pl.BlockSpec(memory_space=pl.ANY)


def call(
    kernel, ins, outs, scratch=(), limit=32, flops=0, where=(), aliases=None, dtype=jnp.float32
):
    return pl.pallas_call(
        kernel,
        out_shape=tuple(jax.ShapeDtypeStruct(s, dtype) for s in outs),
        in_specs=list(ins),
        out_specs=where or (VMEM,) * len(outs),
        scratch_shapes=[
            pltpu.VMEM(s, jnp.float32) if isinstance(s, tuple) else s for s in scratch
        ],
        input_output_aliases=aliases or {},
        compiler_params=pltpu.CompilerParams(vmem_limit_bytes=limit * MIB),
        cost_estimate=pl.CostEstimate(
            flops=flops, bytes_accessed=8 * MIB, transcendentals=0
        ),
    )


def body(count, tracer, offsets, frac_lon, frac_lat, frac_lev, metric, vertical_coef, inverses):
    in_chip = [(i, i ^ 1) for i in range(count)]
    across = [(i, (i - 1 + 2 * (i % 2)) % count) for i in range(count)]
    flat = tracer.reshape(W * R, L)
    pair_out, cross_out = call(edges_kernel, (VMEM,), ((2 * W, L), (2 * W, L)))(flat)
    pair_in = lax.ppermute(pair_out, LAT, in_chip)
    cross_in = lax.ppermute(cross_out, LAT, across)
    fractions = jnp.broadcast_to(
        jnp.concatenate([frac_lat, frac_lev])[:, None], (2 * R, L)
    )
    (begun,) = call(
        mix_core_kernel,
        (VMEM,) * 2,
        ((NL, 2, R, 8, 128),),
        scratch=((5, NL, 2, 8, 128), pltpu.SemaphoreType.DMA((5,))),
        where=(ANY,),
        flops=10**9,
    )(fractions, flat)
    (turned,) = call(
        mix_side_kernel,
        (VMEM,) * 4 + (ANY,),
        ((NL, 2, R, 8, 128),),
        scratch=((3, NL, 2, 8, 128), pltpu.SemaphoreType.DMA((3,))),
        where=(ANY,),
        aliases={4: 0},
    )(fractions, flat, cross_in, pair_in, begun)
    lines = lax.all_to_all(turned, LON, 0, 0, tiled=True)
    (moved,) = call(
        shift_kernel,
        (SMEM, SMEM, VMEM),
        ((NL, 2 * R + 1, 8, 128),),
        scratch=((R, 2 * B, 8, 128),),
    )(offsets, frac_lon, lines.reshape(B, R, 8, 128))
    back = lax.all_to_all(moved, LON, 0, 0, tiled=True)
    vertical = vertical_coef.reshape(1, L)
    some, cross_out, begun = call(
        turn_kernel,
        (SMEM, VMEM, VMEM, VMEM),
        ((H, E, L), (T + L, L), (EARLY, E, L)),
        scratch=((128, L),),
    )(metric, vertical, inverses, back)
    cross = lax.ppermute(cross_out, LAT, across)
    search, images, totals, edges, early, advected, pair_out = call(
        inner_kernel,
        (SMEM,) + (VMEM,) * 5,
        ((3, R, E, L), (3, R, E, L), (9, 8, L), (R, E, L), (2 * EARLY, E, L), (W * R, L), (T + L, L)),
        scratch=((128, L),),
        flops=2 * 10**9,
    )(metric, vertical, inverses, back, some, begun)
    pair = lax.ppermute(pair_out, LAT, in_chip)
    new_search, new_images, sums = call(
        outer_kernel,
        (SMEM,) + (VMEM,) * 9,
        ((3, R, E, L), (3, R, E, L), (count * NL, L)),
    )(metric, vertical, inverses, edges, pair, cross, early, search, images, totals)
    gathered = lax.all_to_all(sums, LON_LAT, 0, 0, tiled=True)
    pressure, residual = call(
        finish_kernel,
        (VMEM,) * 7,
        ((W * R, L), (W * R, L)),
        scratch=((W * R, L), (W * R, L), pltpu.SemaphoreType.DMA((4, 2))),
        where=(HBM, HBM),
    )(gathered, edges, early, search, images, new_search, new_images)
    return tuple(x.reshape(W, R, L) for x in (advected, pressure, residual))


def solution(mesh):
    count = mesh.shape["lat"]
    split = Mesh(mesh.devices.reshape(4, 4, count // 2, 2), LON_LAT)
    placed = (P(LON, LAT, None), P(LAT), P(LAT), P(LAT), P(LAT), P(LAT), P(), P(LAT, None, None))
    return jax.shard_map(
        functools.partial(body, count),
        mesh=split,
        in_specs=placed,
        out_specs=(P(LON, LAT, None),) * 3,
        check_vma=False,
    )
```

```python
import functools

import jax
import jax.numpy as jnp
from jax import lax
from jax.experimental import pallas as pl
from jax.experimental.pallas import tpu as pltpu
from jax.sharding import Mesh
from jax.sharding import PartitionSpec as P

LON = ("lon_0", "lon_1")
LAT = ("lat_0", "lat_1")
LON_LAT = ("lon_0", "lon_1", "lat_0", "lat_1")
W = 256
R = 8
L = 128
H = 3
E = W + 8
NL = 16
B = 2 * NL
T = H * E
MIB = 1 << 20
CORE = (1, 2, 3, 4, 5)
SIDE = (0, 6, 7)


def weights(f):
    sixth = 1.0 / 6.0
    return (
        -f * (f - 1.0) * (f - 2.0) * sixth,
        (f + 1.0) * (f - 1.0) * (f - 2.0) * 0.5,
        -(f + 1.0) * f * (f - 2.0) * 0.5,
        (f + 1.0) * f * (f - 1.0) * sixth,
    )


def halves(x):
    high = x.astype(jnp.bfloat16)
    return high, (x - high.astype(jnp.float32)).astype(jnp.bfloat16)


def dot_nt(a, b):
    return lax.dot_general(
        a, b, (((1,), (1,)), ((), ())), preferred_element_type=jnp.float32
    )


def row_of(j):
    return pl.ds(j, W, stride=R)


def is_even():
    return lax.axis_index("lat_1") == 0


def at_end():
    place = 2 * lax.axis_index("lat_0") + lax.axis_index("lat_1")
    return (place == 0) | (place == 2 * lax.axis_size("lat_0") - 1)


def edges_kernel(tracer, pair, cross):
    even, end = is_even(), at_end()
    last = tracer[row_of(R - 1), :]
    first = tracer[row_of(0), :]
    second = tracer[row_of(1), :]
    pair[0:W] = jnp.where(even, last, first)
    pair[W : 2 * W] = second
    cross[0:W] = jnp.where(end, 0.0, jnp.where(even, first, last))
    cross[W : 2 * W] = jnp.where(end, 0.0, second)


def mix_rows(rows, row, fractions, out, place):
    delta = lax.broadcasted_iota(jnp.int32, (L, L), 1) - lax.broadcasted_iota(
        jnp.int32, (L, L), 0
    )
    for at, j in enumerate(rows):
        w = weights(fractions[j : j + 1, :])
        mixed = w[0] * row(j - 1) + w[1] * row(j) + w[2] * row(j + 1) + w[3] * row(j + 2)
        v = weights(fractions[R + j : R + j + 1, :])
        table = jnp.zeros((L, L), jnp.float32)
        for m in range(4):
            table = jnp.where(delta == m - 1, v[m], table)
        t_high, t_low = halves(table)
        m_high, m_low = halves(mixed)
        left = jnp.concatenate(
            [
                jnp.concatenate([t_high, t_high], 1),
                jnp.concatenate([t_low, t_low], 1),
            ],
            0,
        )
        both = dot_nt(left, jnp.concatenate([m_high, m_low], 1))
        turned = (both[:L] + both[L:]).reshape(NL, 8, W)
        out[:, 0, place[at]] = turned[:, :, :128]
        out[:, 1, place[at]] = turned[:, :, 128:]


def mix_core_kernel(fractions, tracer, out):
    mix_rows(CORE, lambda k: tracer[row_of(k), :], fractions, out, range(len(CORE)))


def mix_side_kernel(fractions, tracer, cross, pair, begun, out):
    even = is_even()

    def row(k):
        if k < 0:
            return jnp.where(even, cross[0:W], pair[0:W])
        if k >= R:
            part = slice((k - R) * W, (k - R + 1) * W)
            return jnp.where(even, pair[part], cross[part])
        return tracer[row_of(k), :]

    for at, j in enumerate(CORE):
        out[:, :, j] = begun[:, :, at]
    mix_rows(SIDE, row, fractions, out, SIDE)


def shift_kernel(offsets, frac_lon, cells, out, twice):
    delta = lax.broadcasted_iota(jnp.int32, (128, 128), 0) - lax.broadcasted_iota(
        jnp.int32, (128, 128), 1
    )
    lane = lax.broadcasted_iota(jnp.int32, (1, 1, 128), 2)
    rims = jnp.zeros((NL, 8, 128), jnp.float32)
    for j in range(R):
        w = weights(frac_lon[j])
        off = offsets[j]
        turns = lax.shift_right_logical(off, 7)
        rest = jnp.bitwise_and(off, 127)
        placed = delta + rest
        left, right_high, right_low = [], [], []
        for k in range(3):
            table = jnp.zeros((128, 128), jnp.float32)
            for m in range(4):
                table = jnp.where(placed == m - 1 - 128 * (k - 1), w[m], table)
            t_high, t_low = halves(table)
            right_high += [t_high, t_high]
            right_low += [t_low, t_low]
            if k == 0:
                part = jnp.concatenate([cells[B - 1 :, j], cells[: B - 1, j]], 0)
            elif k == 1:
                part = cells[:, j]
            else:
                part = jnp.concatenate([cells[1:, j], cells[:1, j]], 0)
            left += list(halves(part.reshape(B * 8, 128)))
        right = jnp.concatenate(
            [jnp.concatenate(right_high, 0), jnp.concatenate(right_low, 0)], 1
        )
        both = jnp.dot(
            jnp.concatenate(left, 1), right, preferred_element_type=jnp.float32
        )
        value = (both[:, :128] + both[:, 128:]).reshape(B, 8, 128)
        twice[j, :B] = value
        twice[j, B:] = value
        start = jnp.bitwise_and(B - turns, B - 1)
        moved = twice[j, pl.ds(start, B)].reshape(NL, 2, 8, 128)
        near, far = moved[:, 0], moved[:, 1]
        out[:, j] = near
        out[:, R + j] = far
        east = jnp.concatenate([near[1:], near[:1]], 0)
        west = jnp.concatenate([far[NL - 1 :], far[: NL - 1]], 0)
        rim = jnp.where(lane < 64, east, west)
        if j > 0:
            rim = pltpu.roll(rim, 8 * j, 2)
        rims = jnp.where(jnp.bitwise_and(lane + (4 - 8 * j), 127) < 8, rim, rims)
    out[:, 2 * R] = rims


def turned_row(cells, rim, j, ref, at):
    sub = lax.broadcasted_iota(jnp.int32, (8, L), 0)
    for h in range(2):
        ref[at, h * 128 : (h + 1) * 128, :] = cells[:, h * R + j].reshape(L, 128).T
    here = pl.multiple_of(8 * j, 8)
    before = pl.multiple_of(jnp.bitwise_and(8 * j + 120, 127), 8)
    ref[at, W:E, :] = jnp.where(sub < 4, rim[pl.ds(here, 8), :], rim[pl.ds(before, 8), :])


def vertical_rows(vertical):
    lane = lax.broadcasted_iota(jnp.int32, (1, L), 1)
    coef = vertical[...]
    return coef, jnp.where(lane == L - 1, 0.0, coef), jnp.where(lane == 0, 0.0, coef)


def precondition(inverse, value):
    m_high, m_low = halves(inverse)
    v_high, v_low = halves(value)
    right = jnp.concatenate(
        [
            jnp.concatenate([m_high, m_high], 1),
            jnp.concatenate([m_low, m_low], 1),
        ],
        0,
    )
    both = dot_nt(jnp.concatenate([v_high, v_low], 1), right)
    return both[:, :L] + both[:, L:]


def alone(q, m, rows):
    coef, upper, lower = rows
    result = q * (2.0 * m + 2.0 * coef + 2.1)
    result = result - m * (pltpu.roll(q, 1, 0) + pltpu.roll(q, E - 1, 0))
    result = result - upper * pltpu.roll(q, L - 1, 1)
    return result - lower * pltpu.roll(q, 1, 1)


def operate(q, south, north, m, rows):
    return alone(q, m, rows) - (south + north)


def metric_row(metric, j):
    return jnp.full((1, L), metric[j], jnp.float32)


Q1 = {0: 0, 1: 1, 2: 2, 7: 8, 6: 9, 5: 10}
V1 = {1: 4, 6: 12}
Q2 = {1: 6, 6: 14}
EARLY = 8


def row_at(end, k):
    return jnp.where(end == 0, k, R - 1 - k)


def solve_end(end, metric, rows, inverses, cells, rim, ring, at, early, base):
    j = [row_at(end, k) for k in range(H)]
    for k in range(H):
        turned_row(cells, rim, j[k], ring, at(k))
        early[base + k] = precondition(inverses[j[k]], ring[at(k)])
    m0, m1 = metric_row(metric, j[0]), metric_row(metric, j[1])
    early[base + 3] = alone(early[base], m0, rows) - early[base + 1]
    early[base + 4] = operate(early[base + 1], early[base], early[base + 2], m1, rows)
    early[base + 5] = precondition(inverses[j[0]], early[base + 3])
    early[base + 6] = precondition(inverses[j[1]], early[base + 4])
    early[base + 7] = alone(early[base + 5], m0, rows) - early[base + 6]


def fill(out, end, metric, inverses, early, base, blank=None):
    j = row_at(end, 0)
    sent = [(n * E, E, early[base + k]) for n, k in enumerate((0, 5, 7))]
    sent += [(T, L, inverses[j]), (W + 3, 1, metric_row(metric, j))]
    for start, size, value in sent:
        value = value if blank is None else jnp.where(blank, 0.0, value)
        out[start : start + size] = value


def turn_kernel(metric, vertical, inverses, cells, ring, cross, pair, early, rim):
    rim[...] = cells[:, 2 * R].reshape(L, 128).T
    rows = vertical_rows(vertical)
    for end, out, blank in ((across_end(), cross, at_end()), (1 - across_end(), pair, None)):
        solve_end(
            end, metric, rows, inverses, cells, rim, ring,
            lambda k, end=end: row_at(end, k), early, EARLY * end,
        )
        fill(out, end, metric, inverses, early, EARLY * end, blank)


def partial(a, b):
    return jnp.sum((a[:W] * b[:W]).reshape(W // 8, 8, L), 0)


def gram(depth, other):
    return 3 + depth * (depth + 1) // 2 + other


def tally(sums, depth, first, images, result):
    sums[depth] = sums[depth] + partial(first, result)
    for other in range(depth):
        k = gram(depth, other)
        sums[k] = sums[k] + partial(images[other], result)
    k = gram(depth, depth)
    sums[k] = sums[k] + partial(result, result)


def direction_of(search, early, depth, j):
    if depth == 0 and j in Q1:
        return (early, Q1[j])
    return (early, Q2[j]) if depth == 1 and j in Q2 else (search, depth, j)


def image_of(field, early, depth, j):
    return (early, V1[j]) if depth == 0 and j in V1 else (field, depth, j)


def read(place, *more):
    return place[0][(*place[1:], *more)]


def inner_kernel(
    metric, vertical, inverses, cells, turned, early, search, field, totals, ring, advected, rim
):
    rows = vertical_rows(vertical)
    rim[...] = cells[:, 2 * R].reshape(L, 128).T
    for j in range(R):
        if H <= j < R - H:
            turned_row(cells, rim, j, ring, j)
        else:
            ring[j] = turned[j]
        advected[row_of(j), :] = ring[j, :W]
    sums = [jnp.zeros((8, L), jnp.float32) for _ in range(9)]

    def q(depth, j):
        return read(direction_of(search, early, depth, j))

    def v(depth, j):
        return read(image_of(field, early, depth, j))

    for depth, solved, applied in ((0, (3, 4), range(2, 6)), (1, range(2, 6), range(2, 6)), (2, range(2, 6), (3, 4))):
        for j in solved:
            search[depth, j] = precondition(
                inverses[j], ring[j] if depth == 0 else v(depth - 1, j)
            )
        for j in applied:
            field[depth, j] = operate(
                q(depth, j), q(depth, j - 1), q(depth, j + 1), metric_row(metric, j), rows
            )
        for j in (1, *applied, 6) if depth == 0 else applied:
            tally(sums, depth, ring[j], [v(o, j) for o in range(depth)], v(depth, j))
    for k in range(9):
        totals[k] = sums[k]


def across_end():
    return jnp.where(is_even(), 0, 1)


def end_sums(end, metric, vertical, inverses, halo, edges, early, search, field, totals, new_q, new_v):
    rows = vertical_rows(vertical)
    base = EARLY * end
    e, i, i2, i3 = (row_at(end, k) for k in range(4))
    m0, m1, m2 = (metric_row(metric, j) for j in (e, i, i2))
    sums = [totals[k] for k in range(9)]
    inverse = halo[T : T + L]
    extra = precondition(inverse, early[base])
    new_v[0] = early[base + 3] - halo[0:E]
    tally(sums, 0, edges[e], (), new_v[0])
    new_q[0] = precondition(inverses[e], new_v[0])
    new_v[1] = operate(new_q[0], early[base + 6], halo[E : 2 * E] - extra, m0, rows)
    tally(sums, 1, edges[e], (new_v[0],), new_v[1])
    new_v[2] = operate(early[base + 6], new_q[0], search[1, i2], m1, rows)
    tally(sums, 1, edges[i], (early[base + 4],), new_v[2])
    outside = halo[2 * E : 3 * E] - alone(extra, halo[W + 3 : W + 4], rows) - new_q[0]
    outside = precondition(inverse, outside)
    new_q[1] = precondition(inverses[e], new_v[1])
    new_q[2] = precondition(inverses[i], new_v[2])
    new_v[3] = operate(new_q[1], new_q[2], outside, m0, rows)
    tally(sums, 2, edges[e], (new_v[0], new_v[1]), new_v[3])
    new_v[4] = operate(new_q[2], new_q[1], search[2, i2], m1, rows)
    tally(sums, 2, edges[i], (early[base + 4], new_v[2]), new_v[4])
    new_v[5] = operate(search[2, i2], new_q[2], search[2, i3], m2, rows)
    tally(sums, 2, edges[i2], (field[0, i2], field[1, i2]), new_v[5])
    return sums


def chip_end_kernel(
    metric, vertical, inverses, halo, edges, early, search, field, totals, new_q, new_v, more
):
    sums = end_sums(
        1 - across_end(), metric, vertical, inverses, halo, edges, early, search, field,
        totals, new_q, new_v,
    )
    for k in range(9):
        more[k] = sums[k]


def far_end_kernel(
    metric, vertical, inverses, halo, edges, early, search, field, totals, new_q, new_v, sums_out
):
    lane = lax.broadcasted_iota(jnp.int32, (1, L), 1)
    sums = end_sums(
        across_end(), metric, vertical, inverses, halo, edges, early, search, field,
        totals, new_q, new_v,
    )
    row = jnp.zeros((1, L), jnp.float32)
    for k in range(9):
        total = jnp.sum(jnp.sum(sums[k], 0, keepdims=True), 1, keepdims=True)
        row = jnp.where(lane == k, total, row)
    sums_out[...] = jnp.broadcast_to(row, sums_out.shape)


def finish_kernel(
    sums, edges, early, search, field, chip_q, chip_v, far_q, far_v, pressure, residual,
    held, left, sems,
):
    lane = lax.broadcasted_iota(jnp.int32, (1, L), 1)
    row = jnp.sum(sums[...], 0, keepdims=True)

    def entry(index):
        value = jnp.sum(jnp.where(lane == index, row, 0.0), 1, keepdims=True)
        return jnp.broadcast_to(value, (1, L))

    b1, b2, b3, g11, g12, g22, g13, g23, g33 = (entry(i) for i in range(9))
    l21 = g12 / g11
    l31 = g13 / g11
    d2 = g22 - l21 * g12
    cross = g23 - l21 * g13
    l32 = cross / d2
    d3 = g33 - l31 * g13 - l32 * cross
    c2 = b2 - l21 * b1
    y1 = b1 / g11
    y2 = c2 / d2
    y3 = (b3 - l31 * b1 - l32 * c2) / d3
    k3 = y3
    k2 = y2 - l32 * k3
    k1 = y1 - l21 * k2 - l31 * k3
    parts = 8
    size = W // parts
    copies = []
    for part in range(parts):
        span = slice(part * size, (part + 1) * size)
        work = [
            (
                j,
                ((search, 0, j), (search, 1, j), (search, 2, j)),
                ((field, 0, j), (field, 1, j), (field, 2, j)),
            )
            for j in range(H, R - H)
        ]
        for end, new_q, new_v in (
            (across_end(), far_q, far_v),
            (1 - across_end(), chip_q, chip_v),
        ):
            base = EARLY * end
            for n in range(H):
                j = row_at(end, n)
                q = (
                    (early, base + n),
                    ((new_q, 0), (early, base + 6), (search, 1, j))[n],
                    ((new_q, 1), (new_q, 2), (search, 2, j))[n],
                )
                v = (
                    ((new_v, 0), (early, base + 4), (field, 0, j))[n],
                    ((new_v, 1), (new_v, 2), (field, 1, j))[n],
                    (new_v, 3 + n),
                )
                work.append((j, q, v))
        for j, places_q, places_v in work:
            q = [read(place, span) for place in places_q]
            v = [read(place, span) for place in places_v]
            to = pl.ds(part * size * R + j, size, stride=R)
            held[to, :] = k1 * q[0] + k2 * q[1] + k3 * q[2]
            left[to, :] = edges[j, span] - k1 * v[0] - k2 * v[1] - k3 * v[2]
        block = pl.ds(part * size * R, size * R)
        for i, (source, target) in enumerate(((held, pressure), (left, residual))):
            copy = pltpu.make_async_copy(
                source.at[block, :], target.at[block, :], sems.at[part, i]
            )
            copy.start()
            copies.append(copy)
    for copy in copies:
        copy.wait()


VMEM = pl.BlockSpec(memory_space=pltpu.VMEM)
SMEM = pl.BlockSpec(memory_space=pltpu.SMEM)
HBM = pl.BlockSpec(memory_space=pltpu.HBM)
ANY = pl.BlockSpec(memory_space=pl.ANY)


def call(
    kernel, ins, outs, scratch=(), limit=32, flops=0, size=8 * MIB, where=(), aliases=None, dtype=jnp.float32
):
    return pl.pallas_call(
        kernel,
        out_shape=tuple(jax.ShapeDtypeStruct(s, dtype) for s in outs),
        in_specs=list(ins),
        out_specs=where or (VMEM,) * len(outs),
        scratch_shapes=[
            pltpu.VMEM(s, jnp.float32) if isinstance(s, tuple) else s for s in scratch
        ],
        input_output_aliases=aliases or {},
        compiler_params=pltpu.CompilerParams(vmem_limit_bytes=limit * MIB),
        cost_estimate=pl.CostEstimate(
            flops=flops, bytes_accessed=size, transcendentals=0
        ),
    )


def body(count, tracer, offsets, frac_lon, frac_lat, frac_lev, metric, vertical_coef, inverses):
    in_chip = [(i, i ^ 1) for i in range(count)]
    across = [(i, (i - 1 + 2 * (i % 2)) % count) for i in range(count)]
    flat = tracer.reshape(W * R, L)
    pair_out, cross_out = call(edges_kernel, (VMEM,), ((2 * W, L), (2 * W, L)))(flat)
    pair_in = lax.ppermute(pair_out, LAT, in_chip)
    cross_in = lax.ppermute(cross_out, LAT, across)
    fractions = jnp.broadcast_to(
        jnp.concatenate([frac_lat, frac_lev])[:, None], (2 * R, L)
    )
    (begun,) = call(
        mix_core_kernel, (VMEM,) * 2, ((NL, 2, len(CORE), 8, 128),), flops=10**9
    )(fractions, flat)
    (turned,) = call(mix_side_kernel, (VMEM,) * 5, ((NL, 2, R, 8, 128),))(
        fractions, flat, cross_in, pair_in, begun
    )
    lines = lax.all_to_all(turned, LON, 0, 0, tiled=True)
    (moved,) = call(
        shift_kernel,
        (SMEM, SMEM, VMEM),
        ((NL, 2 * R + 1, 8, 128),),
        scratch=((R, 2 * B, 8, 128),),
    )(offsets, frac_lon, lines.reshape(B, R, 8, 128))
    back = lax.all_to_all(moved, LON, 0, 0, tiled=True)
    vertical = vertical_coef.reshape(1, L)
    some, cross_out, pair_out, early = call(
        turn_kernel,
        (SMEM, VMEM, VMEM, VMEM),
        ((R, E, L), (T + L, L), (T + L, L), (2 * EARLY, E, L)),
        scratch=((128, L),),
    )(metric, vertical, inverses, back)
    cross = lax.ppermute(cross_out, LAT, across)
    pair = lax.ppermute(pair_out, LAT, in_chip)
    search, images, totals, edges, advected = call(
        inner_kernel,
        (SMEM,) + (VMEM,) * 5,
        ((3, R, E, L), (3, R, E, L), (9, 8, L), (R, E, L), (W * R, L)),
        scratch=((128, L),),
        flops=10**10,
    )(metric, vertical, inverses, back, some, early)
    shared = (metric, vertical, inverses)
    known = (edges, early, search, images)
    specs = (SMEM,) + (VMEM,) * 8
    chip_q, chip_v, totals = call(
        chip_end_kernel, specs, ((3, E, L), (6, E, L), (9, 8, L)), size=4096
    )(*shared, pair, *known, totals)
    far_q, far_v, sums = call(
        far_end_kernel, specs, ((3, E, L), (6, E, L), (count * NL, L))
    )(*shared, cross, *known, totals)
    gathered = lax.all_to_all(sums, LON_LAT, 0, 0, tiled=True)
    pressure, residual = call(
        finish_kernel,
        (VMEM,) * 9,
        ((W * R, L), (W * R, L)),
        scratch=((W * R, L), (W * R, L), pltpu.SemaphoreType.DMA((8, 2))),
        where=(HBM, HBM),
    )(gathered, *known, chip_q, chip_v, far_q, far_v)
    return tuple(x.reshape(W, R, L) for x in (advected, pressure, residual))


def solution(mesh):
    count = mesh.shape["lat"]
    split = Mesh(mesh.devices.reshape(4, 4, count // 2, 2), LON_LAT)
    placed = (P(LON, LAT, None), P(LAT), P(LAT), P(LAT), P(LAT), P(LAT), P(), P(LAT, None, None))
    return jax.shard_map(
        functools.partial(body, count),
        mesh=split,
        in_specs=placed,
        out_specs=(P(LON, LAT, None),) * 3,
        check_vma=False,
    )
```

```python
import functools

import jax
import jax.numpy as jnp
from jax import lax
from jax.experimental import pallas as pl
from jax.experimental.pallas import tpu as pltpu
from jax.sharding import Mesh
from jax.sharding import PartitionSpec as P

LON = ("lon_0", "lon_1")
LAT = ("lat_0", "lat_1")
LON_LAT = ("lon_0", "lon_1", "lat_0", "lat_1")
W = 256
R = 8
L = 128
H = 3
E = W + 8
NL = 16
B = 2 * NL
T = H * E
MIB = 1 << 20
CORE = (1, 2, 3, 4, 5)
SIDE = (0, 6, 7)


def weights(f):
    sixth = 1.0 / 6.0
    return (
        -f * (f - 1.0) * (f - 2.0) * sixth,
        (f + 1.0) * (f - 1.0) * (f - 2.0) * 0.5,
        -(f + 1.0) * f * (f - 2.0) * 0.5,
        (f + 1.0) * f * (f - 1.0) * sixth,
    )


def halves(x):
    high = x.astype(jnp.bfloat16)
    return high, (x - high.astype(jnp.float32)).astype(jnp.bfloat16)


def dot_nt(a, b):
    return lax.dot_general(
        a, b, (((1,), (1,)), ((), ())), preferred_element_type=jnp.float32
    )


def row_of(j):
    return pl.ds(j, W, stride=R)


def is_even():
    return lax.axis_index("lat_1") == 0


def at_end():
    place = 2 * lax.axis_index("lat_0") + lax.axis_index("lat_1")
    return (place == 0) | (place == 2 * lax.axis_size("lat_0") - 1)


def edges_kernel(tracer, pair, cross):
    even, end = is_even(), at_end()
    last = tracer[row_of(R - 1), :]
    first = tracer[row_of(0), :]
    second = tracer[row_of(1), :]
    pair[0:W] = jnp.where(even, last, first)
    pair[W : 2 * W] = second
    cross[0:W] = jnp.where(end, 0.0, jnp.where(even, first, last))
    cross[W : 2 * W] = jnp.where(end, 0.0, second)


def mix_rows(rows, row, fractions, out, place):
    delta = lax.broadcasted_iota(jnp.int32, (L, L), 1) - lax.broadcasted_iota(
        jnp.int32, (L, L), 0
    )
    for at, j in enumerate(rows):
        w = weights(fractions[j : j + 1, :])
        mixed = w[0] * row(j - 1) + w[1] * row(j) + w[2] * row(j + 1) + w[3] * row(j + 2)
        v = weights(fractions[R + j : R + j + 1, :])
        table = jnp.zeros((L, L), jnp.float32)
        for m in range(4):
            table = jnp.where(delta == m - 1, v[m], table)
        t_high, t_low = halves(table)
        m_high, m_low = halves(mixed)
        left = jnp.concatenate(
            [
                jnp.concatenate([t_high, t_high], 1),
                jnp.concatenate([t_low, t_low], 1),
            ],
            0,
        )
        both = dot_nt(left, jnp.concatenate([m_high, m_low], 1))
        turned = (both[:L] + both[L:]).reshape(NL, 8, W)
        out[:, 0, place[at]] = turned[:, :, :128]
        out[:, 1, place[at]] = turned[:, :, 128:]


def mix_core_kernel(fractions, tracer, out):
    mix_rows(CORE, lambda k: tracer[row_of(k), :], fractions, out, range(len(CORE)))


def mix_side_kernel(fractions, tracer, cross, pair, begun, out):
    even = is_even()

    def row(k):
        if k < 0:
            return jnp.where(even, cross[0:W], pair[0:W])
        if k >= R:
            part = slice((k - R) * W, (k - R + 1) * W)
            return jnp.where(even, pair[part], cross[part])
        return tracer[row_of(k), :]

    for at, j in enumerate(CORE):
        out[:, :, j] = begun[:, :, at]
    mix_rows(SIDE, row, fractions, out, SIDE)


def shift_kernel(offsets, frac_lon, cells, out, twice):
    delta = lax.broadcasted_iota(jnp.int32, (128, 128), 0) - lax.broadcasted_iota(
        jnp.int32, (128, 128), 1
    )
    lane = lax.broadcasted_iota(jnp.int32, (1, 1, 128), 2)
    rims = jnp.zeros((NL, 8, 128), jnp.float32)
    for j in range(R):
        w = weights(frac_lon[j])
        off = offsets[j]
        turns = lax.shift_right_logical(off, 7)
        rest = jnp.bitwise_and(off, 127)
        placed = delta + rest
        left, right_high, right_low = [], [], []
        shared = jnp.where(rest < 2, 64, 0)
        for k in range(2):
            table = jnp.zeros((128, 128), jnp.float32)
            for m in range(4):
                if k == 0:
                    table = jnp.where(placed == m - 1 + 128, w[m], table)
                    table = jnp.where(placed == m - 1 - 128, w[m], table)
                else:
                    table = jnp.where(placed == m - 1, w[m], table)
            t_high, t_low = halves(table)
            right_high += [t_high, t_high]
            right_low += [t_low, t_low]
            if k == 0:
                before = jnp.concatenate([cells[B - 1 :, j], cells[: B - 1, j]], 0)
                after = jnp.concatenate([cells[1:, j], cells[:1, j]], 0)
                part = jnp.where(lane < shared, after, before)
            else:
                part = cells[:, j]
            left += list(halves(part.reshape(B * 8, 128)))
        right = jnp.concatenate(
            [jnp.concatenate(right_high, 0), jnp.concatenate(right_low, 0)], 1
        )
        both = jnp.dot(
            jnp.concatenate(left, 1), right, preferred_element_type=jnp.float32
        )
        value = (both[:, :128] + both[:, 128:]).reshape(B, 8, 128)
        twice[j, :B] = value
        twice[j, B:] = value
        start = jnp.bitwise_and(B - turns, B - 1)
        moved = twice[j, pl.ds(start, B)].reshape(NL, 2, 8, 128)
        near, far = moved[:, 0], moved[:, 1]
        out[:, j] = near
        out[:, R + j] = far
        east = jnp.concatenate([near[1:], near[:1]], 0)
        west = jnp.concatenate([far[NL - 1 :], far[: NL - 1]], 0)
        rim = jnp.where(lane < 64, east, west)
        if j > 0:
            rim = pltpu.roll(rim, 8 * j, 2)
        rims = jnp.where(jnp.bitwise_and(lane + (4 - 8 * j), 127) < 8, rim, rims)
    out[:, 2 * R] = rims


def turned_row(cells, rim, j, ref, at):
    sub = lax.broadcasted_iota(jnp.int32, (8, L), 0)
    for h in range(2):
        ref[at, h * 128 : (h + 1) * 128, :] = cells[:, h * R + j].reshape(L, 128).T
    here = pl.multiple_of(8 * j, 8)
    before = pl.multiple_of(jnp.bitwise_and(8 * j + 120, 127), 8)
    ref[at, W:E, :] = jnp.where(sub < 4, rim[pl.ds(here, 8), :], rim[pl.ds(before, 8), :])


def vertical_rows(vertical):
    lane = lax.broadcasted_iota(jnp.int32, (1, L), 1)
    coef = vertical[...]
    return coef, jnp.where(lane == L - 1, 0.0, coef), jnp.where(lane == 0, 0.0, coef)


def precondition(inverse, value):
    m_high, m_low = halves(inverse)
    v_high, v_low = halves(value)
    right = jnp.concatenate(
        [
            jnp.concatenate([m_high, m_high], 1),
            jnp.concatenate([m_low, m_low], 1),
        ],
        0,
    )
    both = dot_nt(jnp.concatenate([v_high, v_low], 1), right)
    return both[:, :L] + both[:, L:]


def alone(q, m, rows):
    coef, upper, lower = rows
    result = q * (2.0 * m + 2.0 * coef + 2.1)
    result = result - m * (pltpu.roll(q, 1, 0) + pltpu.roll(q, E - 1, 0))
    result = result - upper * pltpu.roll(q, L - 1, 1)
    return result - lower * pltpu.roll(q, 1, 1)


def operate(q, south, north, m, rows):
    return alone(q, m, rows) - (south + north)


def metric_row(metric, j):
    return jnp.full((1, L), metric[j], jnp.float32)


Q1 = {0: 0, 1: 1, 2: 2, 7: 8, 6: 9, 5: 10}
V1 = {1: 4, 6: 12}
Q2 = {1: 6, 6: 14}
EARLY = 8


def row_at(end, k):
    return jnp.where(end == 0, k, R - 1 - k)


def solve_end(end, metric, rows, inverses, cells, rim, ring, at, early, base):
    j = [row_at(end, k) for k in range(H)]
    for k in range(H):
        turned_row(cells, rim, j[k], ring, at(k))
        early[base + k] = precondition(inverses[j[k]], ring[at(k)])
    m0, m1 = metric_row(metric, j[0]), metric_row(metric, j[1])
    early[base + 3] = alone(early[base], m0, rows) - early[base + 1]
    early[base + 4] = operate(early[base + 1], early[base], early[base + 2], m1, rows)
    early[base + 5] = precondition(inverses[j[0]], early[base + 3])
    early[base + 6] = precondition(inverses[j[1]], early[base + 4])
    early[base + 7] = alone(early[base + 5], m0, rows) - early[base + 6]


def fill(out, end, metric, inverses, early, base, blank=None):
    j = row_at(end, 0)
    sent = [(n * E, E, early[base + k]) for n, k in enumerate((0, 5, 7))]
    sent += [(T, L, inverses[j]), (W + 3, 1, metric_row(metric, j))]
    for start, size, value in sent:
        value = value if blank is None else jnp.where(blank, 0.0, value)
        out[start : start + size] = value


def turn_kernel(metric, vertical, inverses, cells, ring, cross, pair, early, rim):
    rim[...] = cells[:, 2 * R].reshape(L, 128).T
    rows = vertical_rows(vertical)
    for end, out, blank in ((across_end(), cross, at_end()), (1 - across_end(), pair, None)):
        solve_end(
            end, metric, rows, inverses, cells, rim, ring,
            lambda k, end=end: row_at(end, k), early, EARLY * end,
        )
        fill(out, end, metric, inverses, early, EARLY * end, blank)


def partial(a, b):
    return jnp.sum((a[:W] * b[:W]).reshape(W // 8, 8, L), 0)


def gram(depth, other):
    return 3 + depth * (depth + 1) // 2 + other


def tally(sums, depth, first, images, result):
    sums[depth] = sums[depth] + partial(first, result)
    for other in range(depth):
        k = gram(depth, other)
        sums[k] = sums[k] + partial(images[other], result)
    k = gram(depth, depth)
    sums[k] = sums[k] + partial(result, result)


def direction_of(search, early, depth, j):
    if depth == 0 and j in Q1:
        return (early, Q1[j])
    return (early, Q2[j]) if depth == 1 and j in Q2 else (search, depth, j)


def image_of(field, early, depth, j):
    return (early, V1[j]) if depth == 0 and j in V1 else (field, depth, j)


def read(place, *more):
    return place[0][(*place[1:], *more)]


def inner_kernel(
    metric, vertical, inverses, cells, turned, early, search, field, totals, ring, advected, rim
):
    rows = vertical_rows(vertical)
    rim[...] = cells[:, 2 * R].reshape(L, 128).T
    for j in range(R):
        if H <= j < R - H:
            turned_row(cells, rim, j, ring, j)
        else:
            ring[j] = turned[j]
        advected[row_of(j), :] = ring[j, :W]
    sums = [jnp.zeros((8, L), jnp.float32) for _ in range(9)]

    def q(depth, j):
        return read(direction_of(search, early, depth, j))

    def v(depth, j):
        return read(image_of(field, early, depth, j))

    for depth, solved, applied in ((0, (3, 4), range(2, 6)), (1, range(2, 6), range(2, 6)), (2, range(2, 6), (3, 4))):
        for j in solved:
            search[depth, j] = precondition(
                inverses[j], ring[j] if depth == 0 else v(depth - 1, j)
            )
        for j in applied:
            field[depth, j] = operate(
                q(depth, j), q(depth, j - 1), q(depth, j + 1), metric_row(metric, j), rows
            )
        for j in (1, *applied, 6) if depth == 0 else applied:
            tally(sums, depth, ring[j], [v(o, j) for o in range(depth)], v(depth, j))
    for k in range(9):
        totals[k] = sums[k]


def across_end():
    return jnp.where(is_even(), 0, 1)


def end_sums(end, metric, vertical, inverses, halo, edges, early, search, field, totals, new_q, new_v):
    rows = vertical_rows(vertical)
    base = EARLY * end
    e, i, i2, i3 = (row_at(end, k) for k in range(4))
    m0, m1, m2 = (metric_row(metric, j) for j in (e, i, i2))
    sums = [totals[k] for k in range(9)]
    inverse = halo[T : T + L]
    extra = precondition(inverse, early[base])
    new_v[0] = early[base + 3] - halo[0:E]
    tally(sums, 0, edges[e], (), new_v[0])
    new_q[0] = precondition(inverses[e], new_v[0])
    new_v[1] = operate(new_q[0], early[base + 6], halo[E : 2 * E] - extra, m0, rows)
    tally(sums, 1, edges[e], (new_v[0],), new_v[1])
    new_v[2] = operate(early[base + 6], new_q[0], search[1, i2], m1, rows)
    tally(sums, 1, edges[i], (early[base + 4],), new_v[2])
    outside = halo[2 * E : 3 * E] - alone(extra, halo[W + 3 : W + 4], rows) - new_q[0]
    outside = precondition(inverse, outside)
    new_q[1] = precondition(inverses[e], new_v[1])
    new_q[2] = precondition(inverses[i], new_v[2])
    new_v[3] = operate(new_q[1], new_q[2], outside, m0, rows)
    tally(sums, 2, edges[e], (new_v[0], new_v[1]), new_v[3])
    new_v[4] = operate(new_q[2], new_q[1], search[2, i2], m1, rows)
    tally(sums, 2, edges[i], (early[base + 4], new_v[2]), new_v[4])
    new_v[5] = operate(search[2, i2], new_q[2], search[2, i3], m2, rows)
    tally(sums, 2, edges[i2], (field[0, i2], field[1, i2]), new_v[5])
    return sums


def chip_end_kernel(
    metric, vertical, inverses, halo, edges, early, search, field, totals, new_q, new_v, more
):
    sums = end_sums(
        1 - across_end(), metric, vertical, inverses, halo, edges, early, search, field,
        totals, new_q, new_v,
    )
    for k in range(9):
        more[k] = sums[k]


def far_end_kernel(
    metric, vertical, inverses, halo, edges, early, search, field, totals, new_q, new_v, sums_out
):
    lane = lax.broadcasted_iota(jnp.int32, (1, L), 1)
    sums = end_sums(
        across_end(), metric, vertical, inverses, halo, edges, early, search, field,
        totals, new_q, new_v,
    )
    row = jnp.zeros((1, L), jnp.float32)
    for k in range(9):
        total = jnp.sum(jnp.sum(sums[k], 0, keepdims=True), 1, keepdims=True)
        row = jnp.where(lane == k, total, row)
    sums_out[...] = jnp.broadcast_to(row, sums_out.shape)


def finish_kernel(
    sums, edges, early, search, field, chip_q, chip_v, far_q, far_v, pressure, residual,
    held, left, sems,
):
    lane = lax.broadcasted_iota(jnp.int32, (1, L), 1)
    row = jnp.sum(sums[...], 0, keepdims=True)

    def entry(index):
        value = jnp.sum(jnp.where(lane == index, row, 0.0), 1, keepdims=True)
        return jnp.broadcast_to(value, (1, L))

    b1, b2, b3, g11, g12, g22, g13, g23, g33 = (entry(i) for i in range(9))
    l21 = g12 / g11
    l31 = g13 / g11
    d2 = g22 - l21 * g12
    cross = g23 - l21 * g13
    l32 = cross / d2
    d3 = g33 - l31 * g13 - l32 * cross
    c2 = b2 - l21 * b1
    y1 = b1 / g11
    y2 = c2 / d2
    y3 = (b3 - l31 * b1 - l32 * c2) / d3
    k3 = y3
    k2 = y2 - l32 * k3
    k1 = y1 - l21 * k2 - l31 * k3
    parts = 8
    size = W // parts
    copies = []
    for part in range(parts):
        span = slice(part * size, (part + 1) * size)
        work = [
            (
                j,
                ((search, 0, j), (search, 1, j), (search, 2, j)),
                ((field, 0, j), (field, 1, j), (field, 2, j)),
            )
            for j in range(H, R - H)
        ]
        for end, new_q, new_v in (
            (across_end(), far_q, far_v),
            (1 - across_end(), chip_q, chip_v),
        ):
            base = EARLY * end
            for n in range(H):
                j = row_at(end, n)
                q = (
                    (early, base + n),
                    ((new_q, 0), (early, base + 6), (search, 1, j))[n],
                    ((new_q, 1), (new_q, 2), (search, 2, j))[n],
                )
                v = (
                    ((new_v, 0), (early, base + 4), (field, 0, j))[n],
                    ((new_v, 1), (new_v, 2), (field, 1, j))[n],
                    (new_v, 3 + n),
                )
                work.append((j, q, v))
        for j, places_q, places_v in work:
            q = [read(place, span) for place in places_q]
            v = [read(place, span) for place in places_v]
            to = pl.ds(part * size * R + j, size, stride=R)
            held[to, :] = k1 * q[0] + k2 * q[1] + k3 * q[2]
            left[to, :] = edges[j, span] - k1 * v[0] - k2 * v[1] - k3 * v[2]
        block = pl.ds(part * size * R, size * R)
        for i, (source, target) in enumerate(((held, pressure), (left, residual))):
            copy = pltpu.make_async_copy(
                source.at[block, :], target.at[block, :], sems.at[part, i]
            )
            copy.start()
            copies.append(copy)
    for copy in copies:
        copy.wait()


VMEM = pl.BlockSpec(memory_space=pltpu.VMEM)
SMEM = pl.BlockSpec(memory_space=pltpu.SMEM)
HBM = pl.BlockSpec(memory_space=pltpu.HBM)
ANY = pl.BlockSpec(memory_space=pl.ANY)


def call(
    kernel, ins, outs, scratch=(), limit=32, flops=0, size=8 * MIB, where=(), aliases=None, dtype=jnp.float32
):
    return pl.pallas_call(
        kernel,
        out_shape=tuple(jax.ShapeDtypeStruct(s, dtype) for s in outs),
        in_specs=list(ins),
        out_specs=where or (VMEM,) * len(outs),
        scratch_shapes=[
            pltpu.VMEM(s, jnp.float32) if isinstance(s, tuple) else s for s in scratch
        ],
        input_output_aliases=aliases or {},
        compiler_params=pltpu.CompilerParams(vmem_limit_bytes=limit * MIB),
        cost_estimate=pl.CostEstimate(
            flops=flops, bytes_accessed=size, transcendentals=0
        ),
    )


def body(count, tracer, offsets, frac_lon, frac_lat, frac_lev, metric, vertical_coef, inverses):
    in_chip = [(i, i ^ 1) for i in range(count)]
    across = [(i, (i - 1 + 2 * (i % 2)) % count) for i in range(count)]
    flat = tracer.reshape(W * R, L)
    pair_out, cross_out = call(edges_kernel, (VMEM,), ((2 * W, L), (2 * W, L)))(flat)
    pair_in = lax.ppermute(pair_out, LAT, in_chip)
    cross_in = lax.ppermute(cross_out, LAT, across)
    fractions = jnp.broadcast_to(
        jnp.concatenate([frac_lat, frac_lev])[:, None], (2 * R, L)
    )
    (begun,) = call(
        mix_core_kernel, (VMEM,) * 2, ((NL, 2, len(CORE), 8, 128),), flops=10**9
    )(fractions, flat)
    (turned,) = call(mix_side_kernel, (VMEM,) * 5, ((NL, 2, R, 8, 128),))(
        fractions, flat, cross_in, pair_in, begun
    )
    lines = lax.all_to_all(turned, LON, 0, 0, tiled=True)
    (moved,) = call(
        shift_kernel,
        (SMEM, SMEM, VMEM),
        ((NL, 2 * R + 1, 8, 128),),
        scratch=((R, 2 * B, 8, 128),),
    )(offsets, frac_lon, lines.reshape(B, R, 8, 128))
    back = lax.all_to_all(moved, LON, 0, 0, tiled=True)
    vertical = vertical_coef.reshape(1, L)
    some, cross_out, pair_out, early = call(
        turn_kernel,
        (SMEM, VMEM, VMEM, VMEM),
        ((R, E, L), (T + L, L), (T + L, L), (2 * EARLY, E, L)),
        scratch=((128, L),),
    )(metric, vertical, inverses, back)
    cross = lax.ppermute(cross_out, LAT, across)
    pair = lax.ppermute(pair_out, LAT, in_chip)
    search, images, totals, edges, advected = call(
        inner_kernel,
        (SMEM,) + (VMEM,) * 5,
        ((3, R, E, L), (3, R, E, L), (9, 8, L), (R, E, L), (W * R, L)),
        scratch=((128, L),),
        flops=10**10,
    )(metric, vertical, inverses, back, some, early)
    shared = (metric, vertical, inverses)
    known = (edges, early, search, images)
    specs = (SMEM,) + (VMEM,) * 8
    chip_q, chip_v, totals = call(
        chip_end_kernel, specs, ((3, E, L), (6, E, L), (9, 8, L)), size=4096
    )(*shared, pair, *known, totals)
    far_q, far_v, sums = call(
        far_end_kernel, specs, ((3, E, L), (6, E, L), (count * NL, L))
    )(*shared, cross, *known, totals)
    gathered = lax.all_to_all(sums, LON_LAT, 0, 0, tiled=True)
    pressure, residual = call(
        finish_kernel,
        (VMEM,) * 9,
        ((W * R, L), (W * R, L)),
        scratch=((W * R, L), (W * R, L), pltpu.SemaphoreType.DMA((8, 2))),
        where=(HBM, HBM),
    )(gathered, *known, chip_q, chip_v, far_q, far_v)
    return tuple(x.reshape(W, R, L) for x in (advected, pressure, residual))


def solution(mesh):
    count = mesh.shape["lat"]
    split = Mesh(mesh.devices.reshape(4, 4, count // 2, 2), LON_LAT)
    placed = (P(LON, LAT, None), P(LAT), P(LAT), P(LAT), P(LAT), P(LAT), P(), P(LAT, None, None))
    return jax.shard_map(
        functools.partial(body, count),
        mesh=split,
        in_specs=placed,
        out_specs=(P(LON, LAT, None),) * 3,
        check_vma=False,
    )
```

```python
import functools

import jax
import jax.numpy as jnp
from jax import lax
from jax.experimental import pallas as pl
from jax.experimental.pallas import tpu as pltpu
from jax.sharding import Mesh
from jax.sharding import PartitionSpec as P

LON = ("lon_0", "lon_1")
LAT = ("lat_0", "lat_1")
LON_LAT = ("lon_0", "lon_1", "lat_0", "lat_1")
W = 256
R = 8
L = 128
H = 3
E = W + 8
NL = 16
B = 2 * NL
T = H * E
MIB = 1 << 20
CORE = (1, 2, 3, 4, 5)
SIDE = (0, 6, 7)


def weights(f):
    sixth = 1.0 / 6.0
    return (
        -f * (f - 1.0) * (f - 2.0) * sixth,
        (f + 1.0) * (f - 1.0) * (f - 2.0) * 0.5,
        -(f + 1.0) * f * (f - 2.0) * 0.5,
        (f + 1.0) * f * (f - 1.0) * sixth,
    )


def halves(x):
    high = x.astype(jnp.bfloat16)
    return high, (x - high.astype(jnp.float32)).astype(jnp.bfloat16)


def dot_nt(a, b):
    return lax.dot_general(
        a, b, (((1,), (1,)), ((), ())), preferred_element_type=jnp.float32
    )


def row_of(j):
    return pl.ds(j, W, stride=R)


def is_even():
    return lax.axis_index("lat_1") == 0


def at_end():
    place = 2 * lax.axis_index("lat_0") + lax.axis_index("lat_1")
    return (place == 0) | (place == 2 * lax.axis_size("lat_0") - 1)


def edges_kernel(tracer, pair, cross):
    even, end = is_even(), at_end()
    last = tracer[row_of(R - 1), :]
    first = tracer[row_of(0), :]
    second = tracer[row_of(1), :]
    pair[0:W] = jnp.where(even, last, first)
    pair[W : 2 * W] = second
    cross[0:W] = jnp.where(end, 0.0, jnp.where(even, first, last))
    cross[W : 2 * W] = jnp.where(end, 0.0, second)


def mix_rows(rows, row, fractions, out, place):
    delta = lax.broadcasted_iota(jnp.int32, (L, L), 1) - lax.broadcasted_iota(
        jnp.int32, (L, L), 0
    )
    for at, j in enumerate(rows):
        w = weights(fractions[j : j + 1, :])
        mixed = w[0] * row(j - 1) + w[1] * row(j) + w[2] * row(j + 1) + w[3] * row(j + 2)
        v = weights(fractions[R + j : R + j + 1, :])
        table = jnp.zeros((L, L), jnp.float32)
        for m in range(4):
            table = jnp.where(delta == m - 1, v[m], table)
        t_high, t_low = halves(table)
        m_high, m_low = halves(mixed)
        left = jnp.concatenate(
            [
                jnp.concatenate([t_high, t_high], 1),
                jnp.concatenate([t_low, t_low], 1),
            ],
            0,
        )
        both = dot_nt(left, jnp.concatenate([m_high, m_low], 1))
        turned = (both[:L] + both[L:]).reshape(NL, 8, W)
        out[:, 0, place[at]] = turned[:, :, :128]
        out[:, 1, place[at]] = turned[:, :, 128:]


def mix_core_kernel(fractions, tracer, out):
    mix_rows(CORE, lambda k: tracer[row_of(k), :], fractions, out, range(len(CORE)))


def mix_side_kernel(fractions, tracer, cross, pair, begun, out):
    even = is_even()

    def row(k):
        if k < 0:
            return jnp.where(even, cross[0:W], pair[0:W])
        if k >= R:
            part = slice((k - R) * W, (k - R + 1) * W)
            return jnp.where(even, pair[part], cross[part])
        return tracer[row_of(k), :]

    for at, j in enumerate(CORE):
        out[:, :, j] = begun[:, :, at]
    mix_rows(SIDE, row, fractions, out, SIDE)


def shift_kernel(offsets, frac_lon, cells, out, twice):
    delta = lax.broadcasted_iota(jnp.int32, (128, 128), 0) - lax.broadcasted_iota(
        jnp.int32, (128, 128), 1
    )
    lane = lax.broadcasted_iota(jnp.int32, (1, 1, 128), 2)
    rims = jnp.zeros((NL, 8, 128), jnp.float32)
    for j in range(R):
        w = weights(frac_lon[j])
        off = offsets[j]
        turns = lax.shift_right_logical(off, 7)
        rest = jnp.bitwise_and(off, 127)
        placed = delta + rest
        left, right_high, right_low = [], [], []
        shared = jnp.where(rest < 2, 64, 0)
        for k in range(2):
            table = jnp.zeros((128, 128), jnp.float32)
            for m in range(4):
                if k == 0:
                    table = jnp.where(placed == m - 1 + 128, w[m], table)
                    table = jnp.where(placed == m - 1 - 128, w[m], table)
                else:
                    table = jnp.where(placed == m - 1, w[m], table)
            t_high, t_low = halves(table)
            right_high += [t_high, t_high]
            right_low += [t_low, t_low]
            if k == 0:
                before = jnp.concatenate([cells[B - 1 :, j], cells[: B - 1, j]], 0)
                after = jnp.concatenate([cells[1:, j], cells[:1, j]], 0)
                part = jnp.where(lane < shared, after, before)
            else:
                part = cells[:, j]
            left += list(halves(part.reshape(B * 8, 128)))
        right = jnp.concatenate(
            [jnp.concatenate(right_high, 0), jnp.concatenate(right_low, 0)], 1
        )
        both = jnp.dot(
            jnp.concatenate(left, 1), right, preferred_element_type=jnp.float32
        )
        value = (both[:, :128] + both[:, 128:]).reshape(B, 8, 128)
        twice[j, :B] = value
        twice[j, B:] = value
        start = jnp.bitwise_and(B - turns, B - 1)
        moved = twice[j, pl.ds(start, B)].reshape(NL, 2, 8, 128)
        near, far = moved[:, 0], moved[:, 1]
        out[:, j] = near
        out[:, R + j] = far
        east = jnp.concatenate([near[1:], near[:1]], 0)
        west = jnp.concatenate([far[NL - 1 :], far[: NL - 1]], 0)
        rim = jnp.where(lane < 64, east, west)
        if j > 0:
            rim = pltpu.roll(rim, 8 * j, 2)
        rims = jnp.where(jnp.bitwise_and(lane + (4 - 8 * j), 127) < 8, rim, rims)
    out[:, 2 * R] = rims


def turned_row(cells, rim, j, ref, at):
    sub = lax.broadcasted_iota(jnp.int32, (8, L), 0)
    for h in range(2):
        ref[at, h * 128 : (h + 1) * 128, :] = cells[:, h * R + j].reshape(L, 128).T
    here = pl.multiple_of(8 * j, 8)
    before = pl.multiple_of(jnp.bitwise_and(8 * j + 120, 127), 8)
    ref[at, W:E, :] = jnp.where(sub < 4, rim[pl.ds(here, 8), :], rim[pl.ds(before, 8), :])


def vertical_rows(vertical):
    lane = lax.broadcasted_iota(jnp.int32, (1, L), 1)
    coef = vertical[...]
    return coef, jnp.where(lane == L - 1, 0.0, coef), jnp.where(lane == 0, 0.0, coef)


def precondition(inverse, value):
    m_high, m_low = halves(inverse)
    v_high, v_low = halves(value)
    right = jnp.concatenate(
        [
            jnp.concatenate([m_high, m_high], 1),
            jnp.concatenate([m_low, m_low], 1),
        ],
        0,
    )
    both = dot_nt(jnp.concatenate([v_high, v_low], 1), right)
    return both[:, :L] + both[:, L:]


def alone(q, m, rows):
    coef, upper, lower = rows
    result = q * (2.0 * m + 2.0 * coef + 2.1)
    result = result - m * (pltpu.roll(q, 1, 0) + pltpu.roll(q, E - 1, 0))
    result = result - upper * pltpu.roll(q, L - 1, 1)
    return result - lower * pltpu.roll(q, 1, 1)


def operate(q, south, north, m, rows):
    return alone(q, m, rows) - (south + north)


def metric_row(metric, j):
    return jnp.full((1, L), metric[j], jnp.float32)


Q1 = {0: 0, 1: 1, 2: 2, 7: 8, 6: 9, 5: 10}
V1 = {1: 4, 6: 12}
Q2 = {1: 6, 6: 14}
EARLY = 8


def row_at(end, k):
    return jnp.where(end == 0, k, R - 1 - k)


def solve_end(end, metric, rows, inverses, cells, rim, ring, at, early, base):
    j = [row_at(end, k) for k in range(H)]
    q = []
    for k in range(H):
        turned_row(cells, rim, j[k], ring, at(k))
        q.append(precondition(inverses[j[k]], ring[at(k)]))
    m0, m1 = metric_row(metric, j[0]), metric_row(metric, j[1])
    part = alone(q[0], m0, rows) - q[1]
    whole = operate(q[1], q[0], q[2], m1, rows)
    next_part = precondition(inverses[j[0]], part)
    next_whole = precondition(inverses[j[1]], whole)
    last = alone(next_part, m0, rows) - next_whole
    for k, value in enumerate((*q, part, whole, next_part, next_whole, last)):
        early[base + k] = value


def fill(out, end, metric, inverses, early, base, blank=None):
    j = row_at(end, 0)
    sent = [(n * E, E, early[base + k]) for n, k in enumerate((0, 5, 7))]
    sent += [(T, L, inverses[j]), (W + 3, 1, metric_row(metric, j))]
    for start, size, value in sent:
        value = value if blank is None else jnp.where(blank, 0.0, value)
        out[start : start + size] = value


def turn_kernel(metric, vertical, inverses, cells, ring, cross, pair, early, rim):
    rim[...] = cells[:, 2 * R].reshape(L, 128).T
    rows = vertical_rows(vertical)
    for end, out, blank in ((across_end(), cross, at_end()), (1 - across_end(), pair, None)):
        solve_end(
            end, metric, rows, inverses, cells, rim, ring,
            lambda k, end=end: row_at(end, k), early, EARLY * end,
        )
        fill(out, end, metric, inverses, early, EARLY * end, blank)


def partial(a, b):
    return jnp.sum((a[:W] * b[:W]).reshape(W // 8, 8, L), 0)


def gram(depth, other):
    return 3 + depth * (depth + 1) // 2 + other


def tally(sums, depth, first, images, result):
    sums[depth] = sums[depth] + partial(first, result)
    for other in range(depth):
        k = gram(depth, other)
        sums[k] = sums[k] + partial(images[other], result)
    k = gram(depth, depth)
    sums[k] = sums[k] + partial(result, result)


def direction_of(search, early, depth, j):
    if depth == 0 and j in Q1:
        return (early, Q1[j])
    return (early, Q2[j]) if depth == 1 and j in Q2 else (search, depth, j)


def image_of(field, early, depth, j):
    return (early, V1[j]) if depth == 0 and j in V1 else (field, depth, j)


def read(place, *more):
    return place[0][(*place[1:], *more)]


def inner_kernel(
    metric, vertical, inverses, cells, turned, early, search, field, totals, ring, advected, rim
):
    rows = vertical_rows(vertical)
    rim[...] = cells[:, 2 * R].reshape(L, 128).T
    for j in range(R):
        if H <= j < R - H:
            turned_row(cells, rim, j, ring, j)
        else:
            ring[j] = turned[j]
        advected[row_of(j), :] = ring[j, :W]
    sums = [jnp.zeros((8, L), jnp.float32) for _ in range(9)]

    def q(depth, j):
        return read(direction_of(search, early, depth, j))

    def v(depth, j):
        return read(image_of(field, early, depth, j))

    for depth, solved, applied in ((0, (3, 4), range(2, 6)), (1, range(2, 6), range(2, 6)), (2, range(2, 6), (3, 4))):
        for j in solved:
            search[depth, j] = precondition(
                inverses[j], ring[j] if depth == 0 else v(depth - 1, j)
            )
        for j in applied:
            field[depth, j] = operate(
                q(depth, j), q(depth, j - 1), q(depth, j + 1), metric_row(metric, j), rows
            )
        for j in (1, *applied, 6) if depth == 0 else applied:
            tally(sums, depth, ring[j], [v(o, j) for o in range(depth)], v(depth, j))
    for k in range(9):
        totals[k] = sums[k]


def across_end():
    return jnp.where(is_even(), 0, 1)


def end_sums(end, metric, vertical, inverses, halo, edges, early, search, field, totals, new_q, new_v):
    rows = vertical_rows(vertical)
    base = EARLY * end
    e, i, i2, i3 = (row_at(end, k) for k in range(4))
    m0, m1, m2 = (metric_row(metric, j) for j in (e, i, i2))
    sums = [totals[k] for k in range(9)]
    inverse = halo[T : T + L]
    extra = precondition(inverse, early[base])
    new_v[0] = early[base + 3] - halo[0:E]
    tally(sums, 0, edges[e], (), new_v[0])
    new_q[0] = precondition(inverses[e], new_v[0])
    new_v[1] = operate(new_q[0], early[base + 6], halo[E : 2 * E] - extra, m0, rows)
    tally(sums, 1, edges[e], (new_v[0],), new_v[1])
    new_v[2] = operate(early[base + 6], new_q[0], search[1, i2], m1, rows)
    tally(sums, 1, edges[i], (early[base + 4],), new_v[2])
    outside = halo[2 * E : 3 * E] - alone(extra, halo[W + 3 : W + 4], rows) - new_q[0]
    outside = precondition(inverse, outside)
    new_q[1] = precondition(inverses[e], new_v[1])
    new_q[2] = precondition(inverses[i], new_v[2])
    new_v[3] = operate(new_q[1], new_q[2], outside, m0, rows)
    tally(sums, 2, edges[e], (new_v[0], new_v[1]), new_v[3])
    new_v[4] = operate(new_q[2], new_q[1], search[2, i2], m1, rows)
    tally(sums, 2, edges[i], (early[base + 4], new_v[2]), new_v[4])
    new_v[5] = operate(search[2, i2], new_q[2], search[2, i3], m2, rows)
    tally(sums, 2, edges[i2], (field[0, i2], field[1, i2]), new_v[5])
    return sums


def chip_end_kernel(
    metric, vertical, inverses, halo, edges, early, search, field, totals, new_q, new_v, more
):
    sums = end_sums(
        1 - across_end(), metric, vertical, inverses, halo, edges, early, search, field,
        totals, new_q, new_v,
    )
    for k in range(9):
        more[k] = sums[k]


def far_end_kernel(
    metric, vertical, inverses, halo, edges, early, search, field, totals, new_q, new_v, sums_out
):
    lane = lax.broadcasted_iota(jnp.int32, (1, L), 1)
    sums = end_sums(
        across_end(), metric, vertical, inverses, halo, edges, early, search, field,
        totals, new_q, new_v,
    )
    row = jnp.zeros((1, L), jnp.float32)
    for k in range(9):
        total = jnp.sum(jnp.sum(sums[k], 0, keepdims=True), 1, keepdims=True)
        row = jnp.where(lane == k, total, row)
    sums_out[...] = jnp.broadcast_to(row, sums_out.shape)


def finish_kernel(
    sums, edges, early, search, field, chip_q, chip_v, far_q, far_v, pressure, residual,
    held, left, sems,
):
    lane = lax.broadcasted_iota(jnp.int32, (1, L), 1)
    row = jnp.sum(sums[...], 0, keepdims=True)

    def entry(index):
        value = jnp.sum(jnp.where(lane == index, row, 0.0), 1, keepdims=True)
        return jnp.broadcast_to(value, (1, L))

    b1, b2, b3, g11, g12, g22, g13, g23, g33 = (entry(i) for i in range(9))
    l21 = g12 / g11
    l31 = g13 / g11
    d2 = g22 - l21 * g12
    cross = g23 - l21 * g13
    l32 = cross / d2
    d3 = g33 - l31 * g13 - l32 * cross
    c2 = b2 - l21 * b1
    y1 = b1 / g11
    y2 = c2 / d2
    y3 = (b3 - l31 * b1 - l32 * c2) / d3
    k3 = y3
    k2 = y2 - l32 * k3
    k1 = y1 - l21 * k2 - l31 * k3
    parts = 8
    size = W // parts
    copies = []
    for part in range(parts):
        span = slice(part * size, (part + 1) * size)
        work = [
            (
                j,
                ((search, 0, j), (search, 1, j), (search, 2, j)),
                ((field, 0, j), (field, 1, j), (field, 2, j)),
            )
            for j in range(H, R - H)
        ]
        for end, new_q, new_v in (
            (across_end(), far_q, far_v),
            (1 - across_end(), chip_q, chip_v),
        ):
            base = EARLY * end
            for n in range(H):
                j = row_at(end, n)
                q = (
                    (early, base + n),
                    ((new_q, 0), (early, base + 6), (search, 1, j))[n],
                    ((new_q, 1), (new_q, 2), (search, 2, j))[n],
                )
                v = (
                    ((new_v, 0), (early, base + 4), (field, 0, j))[n],
                    ((new_v, 1), (new_v, 2), (field, 1, j))[n],
                    (new_v, 3 + n),
                )
                work.append((j, q, v))
        for j, places_q, places_v in work:
            q = [read(place, span) for place in places_q]
            v = [read(place, span) for place in places_v]
            to = pl.ds(part * size * R + j, size, stride=R)
            held[to, :] = k1 * q[0] + k2 * q[1] + k3 * q[2]
            left[to, :] = edges[j, span] - k1 * v[0] - k2 * v[1] - k3 * v[2]
        block = pl.ds(part * size * R, size * R)
        for i, (source, target) in enumerate(((held, pressure), (left, residual))):
            copy = pltpu.make_async_copy(
                source.at[block, :], target.at[block, :], sems.at[part, i]
            )
            copy.start()
            copies.append(copy)
    for copy in copies:
        copy.wait()


VMEM = pl.BlockSpec(memory_space=pltpu.VMEM)
SMEM = pl.BlockSpec(memory_space=pltpu.SMEM)
HBM = pl.BlockSpec(memory_space=pltpu.HBM)
ANY = pl.BlockSpec(memory_space=pl.ANY)


def call(
    kernel, ins, outs, scratch=(), limit=32, flops=0, size=8 * MIB, where=(), aliases=None, dtype=jnp.float32
):
    return pl.pallas_call(
        kernel,
        out_shape=tuple(jax.ShapeDtypeStruct(s, dtype) for s in outs),
        in_specs=list(ins),
        out_specs=where or (VMEM,) * len(outs),
        scratch_shapes=[
            pltpu.VMEM(s, jnp.float32) if isinstance(s, tuple) else s for s in scratch
        ],
        input_output_aliases=aliases or {},
        compiler_params=pltpu.CompilerParams(vmem_limit_bytes=limit * MIB),
        cost_estimate=pl.CostEstimate(
            flops=flops, bytes_accessed=size, transcendentals=0
        ),
    )


def body(count, tracer, offsets, frac_lon, frac_lat, frac_lev, metric, vertical_coef, inverses):
    in_chip = [(i, i ^ 1) for i in range(count)]
    across = [(i, (i - 1 + 2 * (i % 2)) % count) for i in range(count)]
    flat = tracer.reshape(W * R, L)
    pair_out, cross_out = call(edges_kernel, (VMEM,), ((2 * W, L), (2 * W, L)))(flat)
    pair_in = lax.ppermute(pair_out, LAT, in_chip)
    cross_in = lax.ppermute(cross_out, LAT, across)
    fractions = jnp.broadcast_to(
        jnp.concatenate([frac_lat, frac_lev])[:, None], (2 * R, L)
    )
    (begun,) = call(
        mix_core_kernel, (VMEM,) * 2, ((NL, 2, len(CORE), 8, 128),), flops=10**9
    )(fractions, flat)
    (turned,) = call(mix_side_kernel, (VMEM,) * 5, ((NL, 2, R, 8, 128),))(
        fractions, flat, cross_in, pair_in, begun
    )
    lines = lax.all_to_all(turned, LON, 0, 0, tiled=True)
    (moved,) = call(
        shift_kernel,
        (SMEM, SMEM, VMEM),
        ((NL, 2 * R + 1, 8, 128),),
        scratch=((R, 2 * B, 8, 128),),
    )(offsets, frac_lon, lines.reshape(B, R, 8, 128))
    back = lax.all_to_all(moved, LON, 0, 0, tiled=True)
    vertical = vertical_coef.reshape(1, L)
    some, cross_out, pair_out, early = call(
        turn_kernel,
        (SMEM, VMEM, VMEM, VMEM),
        ((R, E, L), (T + L, L), (T + L, L), (2 * EARLY, E, L)),
        scratch=((128, L),),
    )(metric, vertical, inverses, back)
    cross = lax.ppermute(cross_out, LAT, across)
    pair = lax.ppermute(pair_out, LAT, in_chip)
    search, images, totals, edges, advected = call(
        inner_kernel,
        (SMEM,) + (VMEM,) * 5,
        ((3, R, E, L), (3, R, E, L), (9, 8, L), (R, E, L), (W * R, L)),
        scratch=((128, L),),
        flops=10**10,
    )(metric, vertical, inverses, back, some, early)
    shared = (metric, vertical, inverses)
    known = (edges, early, search, images)
    specs = (SMEM,) + (VMEM,) * 8
    chip_q, chip_v, totals = call(
        chip_end_kernel, specs, ((3, E, L), (6, E, L), (9, 8, L)), size=4096
    )(*shared, pair, *known, totals)
    far_q, far_v, sums = call(
        far_end_kernel, specs, ((3, E, L), (6, E, L), (count * NL, L))
    )(*shared, cross, *known, totals)
    gathered = lax.all_to_all(sums, LON_LAT, 0, 0, tiled=True)
    pressure, residual = call(
        finish_kernel,
        (VMEM,) * 9,
        ((W * R, L), (W * R, L)),
        scratch=((W * R, L), (W * R, L), pltpu.SemaphoreType.DMA((8, 2))),
        where=(HBM, HBM),
    )(gathered, *known, chip_q, chip_v, far_q, far_v)
    return tuple(x.reshape(W, R, L) for x in (advected, pressure, residual))


def solution(mesh):
    count = mesh.shape["lat"]
    split = Mesh(mesh.devices.reshape(4, 4, count // 2, 2), LON_LAT)
    placed = (P(LON, LAT, None), P(LAT), P(LAT), P(LAT), P(LAT), P(LAT), P(), P(LAT, None, None))
    return jax.shard_map(
        functools.partial(body, count),
        mesh=split,
        in_specs=placed,
        out_specs=(P(LON, LAT, None),) * 3,
        check_vma=False,
    )
```
